32 devices in a mesh: groups: 2 (over y), hst: 4 (over z), mp: 2 (over x), rep: 2 (over core).
Axes of the slice: x: 2, y: 2, z: 4, core: 2. Of those that a mesh axis runs over, the one named last changes fastest.
Arguments:
- activations: bfloat16 [4, 1024, 6144], P(None, ('groups', 'hst', 'rep'), 'mp'), parts along dimension 1, may hold values from -6 to 6
- shrink_weight: bfloat16 [128, 16, 6144], P('hst', None, 'mp'), may hold values from -0.078125 to 0.078125
- expand_weight: bfloat16 [128, 16, 6144], P('hst', None, 'mp'), may hold values from -1.5 to 1.5
- former_layout_list: int32 [256], P('groups'), parts along dimension 0, may hold values from 0 to 127, as said below
- host_layout_list: int32 [256], P('groups'), parts along dimension 0, may hold values from 0 to 127, as said below
- target_host: int32 [4, 1024, 1], P(None, ('groups', 'hst', 'rep')), parts along dimension 1, may hold values from 0 to 3; in each aligned block of 64 rows (0 to 63, 64 to 127, ..., all dimensions but the last counted through in order) at most 32 rows name the same one
- target_position: int32 [4, 1024], P(None, ('groups', 'hst', 'rep')), parts along dimension 1, may hold values from 0 to 31
Outputs:
- lora_delta: bfloat16 [4, 1024, 6144], P(None, ('groups', 'hst', 'rep'), 'mp'), parts along dimension 1
The draws below stay inside these ranges and needn't reach their ends.
There are 2 independent parts, one for each index of `groups`. The reference program is written for one: setup_inputs(seed, part) draws one part's arguments, and reference() takes and returns one part's arrays. A program takes and returns all parts, laid end to end along the dimension named above; an argument that names none is the same for every part. Nothing has to cross between parts.
Inputs may be any that keep to these rules, and one draw needn't show every extreme that they name: `former_layout_list`: a permutation of the adapters. `host_layout_list`: positions h * 32 to (h + 1) * 32 - 1 belong to host h; of one host's positions exactly 8 hold adapters whose old positions lie with each owner; an adapter may stand on several hosts. `target_host`: in each step, the 64 requests of one device name one host at most 32 times.
All inputs are finite; a program needn't handle non-finite values.
Results may differ from the reference program's by a relative error of at most 0.0051.
Values may be sent and summed in bfloat16 or wider, within the bound.
No kernel may reach another device: no remote copies, remote signals or barrier semaphores. Data moves between devices by JAX's collectives and lax.ppermute only.
A program may use at most 64 MiB of HBM per device.

```python
import math
import jax
import jax.numpy as jnp
import numpy as np
from jax import lax

MODEL_WIDTH = 6144
ADAPTER_RANK = 16
ADP_HOST = 32
STEPS = 4
REQ_DEV = 64
ADAPTER_TOTAL = 128
REQUESTS = 512
CAP = 32
MOVE = 8
N_HST = 4


def layout(key):
    old_table = jax.random.permutation(jax.random.fold_in(key, 5), ADAPTER_TOTAL).astype(jnp.int32)
    owner_key = jax.random.fold_in(key, 6)
    index_key = jax.random.fold_in(key, 7)

    def host_row(host_id):
        shuffled = jax.random.permutation(jax.random.fold_in(owner_key, host_id), N_HST * MOVE)
        owners = shuffled // MOVE
        first_key, second_key = jax.random.split(jax.random.fold_in(index_key, host_id))
        within = jnp.minimum(jax.random.randint(first_key, (ADP_HOST,), 0, ADP_HOST), jax.random.randint(second_key, (ADP_HOST,), 0, ADP_HOST))
        return owners * ADP_HOST + within
    chosen = jax.vmap(host_row)(jnp.arange(N_HST)).reshape(-1).astype(jnp.int32)
    return (old_table, old_table[chosen].astype(jnp.int32))


def draw_former_layout_list(key, part):
    shared = layout(key)
    return shared[0]


def draw_host_layout_list(key, part):
    shared = layout(key)
    return shared[1]


def plant(values, stream_key, smallest, largest):
    dims = values.shape
    index_at = [jax.random.randint(jax.random.fold_in(stream_key, axis), (), 0, dims[axis]) for axis in range(len(dims))]
    values = values.at[tuple(index_at)].set(smallest)
    longest = dims.index(max(dims))
    index_at[longest] = (index_at[longest] + 1) % dims[longest]
    return values.at[tuple(index_at)].set(largest)


def level_of(stream_key, extent, cuts, smallest, largest):
    def one(dim, blocks):
        draws = jax.random.uniform(jax.random.fold_in(jax.random.fold_in(stream_key, 6), dim), (blocks,), jnp.float32, smallest / len(cuts), largest / len(cuts))
        return jnp.repeat(jnp.exp(draws), extent[dim] // blocks).reshape((-1,) + (1,) * (len(extent) - dim - 1))

    factor_of = one(*cuts[0])
    for cut in cuts[1:]:
        factor_of = factor_of * one(*cut)
    return factor_of


def shared_out(rng, own, number, rows, amount, top, bound, skew):
    sequence = jax.random.permutation(rng, amount)
    packed, usual = portions_of(amount, rows * top, bound, skew, True), portions_of(amount, rows * top, bound, skew, False)
    places = jnp.arange(amount)

    def named(lengths, offset_by):
        used = int((lengths > 0).sum())
        fixed = max(1, used // 4)
        moved = fixed + (places - fixed + offset_by * (used - fixed)) % max(1, amount - fixed)
        return jnp.zeros((amount,), jnp.int32).at[sequence[jnp.where(places < fixed, places, moved)]].set(jnp.asarray(lengths, jnp.int32))

    lengths = jnp.where(number % 4 == 0, named(packed, number // 4), named(usual, number - number // 4 - 1))
    mixed = jax.random.permutation(jax.random.fold_in(own, 3), amount)
    source_of, sink = mixed[0:amount // 2 * 2:2], mixed[1:amount // 2 * 2:2]
    margin = jnp.minimum(lengths[source_of] - 1, bound - lengths[sink]) // 2
    margin = jnp.where((source_of == sequence[0]) | (sink == sequence[0]) | (lengths[sink] == 0), 0, jnp.maximum(margin, 0))
    moved = jax.random.randint(jax.random.fold_in(own, 4), (amount // 2,), 0, 1 << 20) % (margin + 1)
    lengths = lengths.at[source_of].add(-moved).at[sink].add(moved)
    members = jnp.searchsorted(jnp.cumsum(lengths), jnp.arange(rows * top), side="right").astype(jnp.int32)
    grid = members.reshape(top, rows).T
    grid = grid[jax.random.permutation(jax.random.fold_in(own, 1), rows)]
    offset_by = jax.random.randint(jax.random.fold_in(own, 2), (rows, 1), 0, top)
    return jnp.take_along_axis(grid, (jnp.arange(top)[None, :] + offset_by) % top, axis=1)


def portions_of(number_of, total, limit, lean, full):
    loads = [(1 << 20) // math.isqrt(grade ** lean) + 1 for grade in range(1, number_of + 1)]
    largest = limit if full else min(limit, max(-(-total // number_of), total * loads[0] // sum(loads)))
    least = 1 if total - largest >= number_of - 1 else 0
    holding, surplus = [largest] + [least] * (number_of - 1), total - largest - least * (number_of - 1)
    while surplus > 0:
        candidates = [i for i in range(1, number_of) if holding[i] < largest] or [i for i in range(1, number_of) if holding[i] < limit]
        mass, remaining = sum([loads[i] for i in candidates]), surplus
        for i in candidates:
            more = min(limit - holding[i], max(1, remaining * loads[i] // mass), surplus)
            holding[i] = holding[i] + more
            surplus = surplus - more
    return np.array(holding)


def scatter_about(stream_key, dims, spread, most, cuts=(), kind=jnp.bfloat16):
    entries = spread * jax.random.normal(stream_key, dims, jnp.float32)
    if cuts:
        entries = entries * level_of(stream_key, dims, cuts, -0.22, 0.18)
    return jnp.clip(entries, -most, most).astype(kind)


def setup_inputs(seed: int = 0, part: int = 0) -> dict:
    key_of = jax.random.split(jax.random.key(seed), 8)
    part_keys = jax.random.split(jax.random.fold_in(key_of[7], part), 8)
    activations = scatter_about(part_keys[0], (STEPS, REQUESTS, MODEL_WIDTH), 1.0, 6.0, ((1, 8), (2, 2)))
    shrink_weight = scatter_about(key_of[1], (ADAPTER_TOTAL, ADAPTER_RANK, MODEL_WIDTH), MODEL_WIDTH ** -0.5, 0.078125, ((0, 4), (2, 2)))
    expand_weight = scatter_about(key_of[2], (ADAPTER_TOTAL, ADAPTER_RANK, MODEL_WIDTH), ADAPTER_RANK ** -0.5, 1.5, ((0, 4), (2, 2)))
    former_layout_list = draw_former_layout_list(jax.random.fold_in(jax.random.fold_in(key_of[7], part), 71), part)
    host_layout_list = draw_host_layout_list(jax.random.fold_in(jax.random.fold_in(key_of[7], part), 71), part)
    target_host_keys = jax.random.split(jax.random.fold_in(part_keys[5], 1), STEPS * REQUESTS // REQ_DEV)
    target_host_turns = jax.random.permutation(jax.random.fold_in(part_keys[5], 3), STEPS * REQUESTS // REQ_DEV)
    target_host = jax.vmap(lambda own, number: shared_out(jax.random.fold_in(part_keys[5], 2), own, number, REQ_DEV, N_HST, 1, CAP, 2))(target_host_keys, target_host_turns).reshape((STEPS, REQUESTS, 1))
    target_position = plant(jax.random.randint(part_keys[6], (STEPS, REQUESTS), 0, ADP_HOST), jax.random.fold_in(part_keys[6], 1), 0, ADP_HOST - 1).astype(jnp.int32)
    return dict(activations=activations, shrink_weight=shrink_weight, expand_weight=expand_weight, former_layout_list=former_layout_list, host_layout_list=host_layout_list, target_host=target_host, target_position=target_position)


def reference(activations, shrink_weight, expand_weight, former_layout_list, host_layout_list, target_host, target_position):
    position = jnp.argsort(former_layout_list).astype(jnp.int32)
    hosted = position[host_layout_list].astype(jnp.int32)
    served = hosted[(target_host[:, :, 0] * ADP_HOST + target_position).astype(jnp.int32)]
    rows_all = activations.reshape(-1, REQ_DEV, MODEL_WIDTH)
    which_all = served.reshape(-1, REQ_DEV)

    def serve_block(pieces):
        rows_here, local_choice = pieces
        shrink_factor = shrink_weight[local_choice].astype(jnp.float32)
        expand_factor = expand_weight[local_choice].astype(jnp.float32)
        shrink = jnp.einsum('nd,nrd->nr', rows_here.astype(jnp.float32), shrink_factor).astype(jnp.bfloat16)
        return jnp.einsum('nr,nrd->nd', shrink.astype(jnp.float32), expand_factor).astype(jnp.bfloat16)

    result = lax.map(serve_block, (rows_all, which_all))
    return result.reshape(STEPS, REQUESTS, MODEL_WIDTH)
```

```python
import jax
import jax.numpy as jnp
from jax import lax
from jax.sharding import PartitionSpec as P

FIRST_ROUNDS = 2


def local(
    activations,
    shrink_weight,
    expand_weight,
    former_layout_list,
    host_layout_list,
    target_host,
    target_position,
):
    host_count = lax.axis_size("hst")
    shares = lax.axis_size("mp")
    local_adapters, rank_extent, width = shrink_weight.shape
    steps, step_rows, _ = activations.shape
    rows = steps * step_rows
    table_size = former_layout_list.shape[0]
    block = 8 * -(-3 * rows // (4 * host_count * 8))
    slots = block - 1

    flat_x = activations.reshape(rows, width)
    flat_a = shrink_weight.reshape(local_adapters * rank_extent, width)
    flat_b = expand_weight.reshape(local_adapters * rank_extent, width)

    table = jnp.arange(table_size, dtype=jnp.int32)
    source = jnp.sum(
        jnp.where(host_layout_list[:, None] == former_layout_list[None, :], table[None, :], 0),
        axis=1,
    )
    wanted = (target_host[:, :, 0] * local_adapters + target_position).reshape(rows)
    served = jnp.sum(jnp.where(wanted[:, None] == table[None, :], source[None, :], 0), axis=1)
    owner = served // local_adapters
    within = served % local_adapters

    hosts = jnp.arange(host_count, dtype=jnp.int32)
    by_owner = owner[:, None] == hosts[None, :]
    row_ids = jnp.arange(rows, dtype=jnp.int32)
    earlier = (row_ids[None, :] < row_ids[:, None]).astype(jnp.bfloat16)
    before = jnp.dot(
        earlier, by_owner.astype(jnp.bfloat16), preferred_element_type=jnp.float32
    ).astype(jnp.int32)
    row_rank = jnp.sum(jnp.where(by_owner, before, 0), axis=1)
    rounds = lax.pmax(jnp.max(row_rank) // slots + 1, ("groups", "hst", "mp", "rep"))

    place_owner = jnp.repeat(hosts, block)
    place_slot = jnp.tile(jnp.arange(block, dtype=jnp.int32), host_count)
    is_slot = place_slot < slots
    adapters = jnp.arange(local_adapters, dtype=jnp.int32)
    columns = jnp.arange(width, dtype=jnp.int32)

    def place(number):
        chosen = (
            (place_owner[:, None] == owner[None, :])
            & (place_slot[:, None] + number * slots == row_rank[None, :])
            & is_slot[:, None]
        )
        return chosen.astype(jnp.bfloat16)

    def send(number):
        placer = place(number)
        column_slot = number * slots + columns
        named = jnp.sum(
            jnp.where(
                (owner[:, None, None] == hosts[None, :, None])
                & (row_rank[:, None, None] == column_slot[None, None, :slots]),
                (within + 1)[:, None, None],
                0,
            ),
            axis=0,
        )
        named = jnp.pad(named.astype(jnp.float32), ((0, 0), (0, width - slots)))
        sent = jnp.dot(placer, flat_x, preferred_element_type=jnp.float32)
        sent = sent.reshape(host_count, block, width) + jnp.where(
            (jnp.arange(block) == slots)[None, :, None], named[:, None, :], 0.0
        )
        return lax.all_to_all(
            sent.astype(jnp.bfloat16), "hst", split_axis=0, concat_axis=0, tiled=True
        )

    def serve(received):
        named = received[:, slots, :block].astype(jnp.int32)
        named = jnp.where(jnp.arange(block)[None, :] < slots, named, 0).reshape(-1)
        mask = named[:, None] == adapters[None, :] + 1
        partial = lax.dot_general(
            received.reshape(-1, width),
            flat_a,
            (((1,), (1,)), ((), ())),
            preferred_element_type=jnp.float32,
        )
        partial = jnp.sum(
            jnp.where(
                mask[:, :, None], partial.reshape(-1, local_adapters, rank_extent), 0.0
            ),
            axis=1,
        )
        total = partial
        for hop in range(1, shares):
            total = total + lax.ppermute(
                partial, "mp", [(i, (i + hop) % shares) for i in range(shares)]
            )
        shrink = total.astype(jnp.bfloat16)
        spread = jnp.where(mask[:, :, None], shrink[:, None, :], 0).reshape(
            -1, local_adapters * rank_extent
        )
        adapted = jnp.dot(spread, flat_b, preferred_element_type=jnp.float32)
        return lax.all_to_all(
            adapted.astype(jnp.bfloat16).reshape(received.shape),
            "hst",
            split_axis=0,
            concat_axis=0,
            tiled=True,
        )

    def back(number, returned):
        return lax.dot_general(
            place(number),
            returned.reshape(-1, width),
            (((0,), (0,)), ((), ())),
            preferred_element_type=jnp.float32,
        )

    sent = [send(number) for number in range(FIRST_ROUNDS)]
    returned = [serve(received) for received in sent]
    result = back(0, returned[0]).astype(jnp.bfloat16)
    for number in range(1, FIRST_ROUNDS):
        result = (back(number, returned[number]) + result).astype(jnp.bfloat16)

    def more(state):
        number, so_far = state
        added = back(number, serve(send(number)))
        return number + 1, (added + so_far).astype(jnp.bfloat16)

    _, result = lax.while_loop(
        lambda state: state[0] < rounds, more, (jnp.int32(FIRST_ROUNDS), result)
    )
    return result.reshape(steps, step_rows, width)


def solution(mesh):
    return jax.shard_map(
        local,
        mesh=mesh,
        in_specs=(
            P(None, ("groups", "hst", "rep"), "mp"),
            P("hst", None, "mp"),
            P("hst", None, "mp"),
            P("groups"),
            P("groups"),
            P(None, ("groups", "hst", "rep"), None),
            P(None, ("groups", "hst", "rep")),
        ),
        out_specs=P(None, ("groups", "hst", "rep"), "mp"),
        check_vma=False,
    )
```

```python
import jax
import jax.numpy as jnp
from jax import lax
from jax.sharding import PartitionSpec as P

MOST_SHIFTS = 8
LANES = 128


def round_up(value, unit):
    return unit * -(-value // unit)


def local(
    activations,
    shrink_weight,
    expand_weight,
    former_layout_list,
    host_layout_list,
    target_host,
    target_position,
):
    host_count = lax.axis_size("hst")
    shares = lax.axis_size("mp")
    me = lax.axis_index("hst")
    local_adapters, rank_extent, width = shrink_weight.shape
    steps, step_rows, _ = activations.shape
    rows = steps * step_rows
    spots = local_adapters * rank_extent
    folded = LANES if spots % LANES == 0 and LANES % rank_extent == 0 else spots
    table_size = former_layout_list.shape[0]
    by_shift = host_count <= MOST_SHIFTS
    first_block = round_up(11 * rows // (8 * host_count), 8)
    more_block = min(first_block, 16)

    flat_x = activations.reshape(rows, width)
    flat_a = shrink_weight.reshape(spots, width)
    flat_b = expand_weight.reshape(spots, width)

    table = jnp.arange(table_size, dtype=jnp.int32)
    source = jnp.sum(
        jnp.where(host_layout_list[:, None] == former_layout_list[None, :], table[None, :], 0),
        axis=1,
    )
    wanted = (target_host[:, :, 0] * local_adapters + target_position).reshape(rows)
    served = jnp.sum(jnp.where(wanted[:, None] == table[None, :], source[None, :], 0), axis=1)
    owner = served // local_adapters
    named_row = served % local_adapters + 1
    ahead = lax.rem(owner - me + host_count, host_count)
    key = ahead if by_shift else jnp.where(ahead == 0, host_count, owner)

    hosts = jnp.arange(host_count, dtype=jnp.int32)
    in_block = key[:, None] == hosts[None, :]
    row_ids = jnp.arange(rows, dtype=jnp.int32)
    earlier = (row_ids[None, :] < row_ids[:, None]).astype(jnp.bfloat16)
    before = jnp.dot(
        earlier, in_block.astype(jnp.bfloat16), preferred_element_type=jnp.float32
    ).astype(jnp.int32)
    row_rank = jnp.sum(jnp.where(in_block, before, 0), axis=1)
    left = jnp.max(jnp.where(ahead == 0, 0, row_rank + 1)) - (first_block - 1)
    own_rounds = jnp.maximum(0, (left + more_block - 2) // (more_block - 1))

    columns = jnp.arange(width, dtype=jnp.int32)
    spot_adapter = jnp.arange(spots, dtype=jnp.int32) // rank_extent + 1

    def place(member, start, block):
        slot = jnp.arange(block, dtype=jnp.int32)[:, None]
        chosen = (
            (key[None, :] == member)
            & (slot + start == row_rank[None, :])
            & (slot < block - 1)
        )
        return chosen

    def pack(member, start, block):
        chosen = place(member, start, block)
        at_column = (key[:, None] == member) & (row_rank[:, None] == columns[None, :LANES] + start)
        names = jnp.sum(jnp.where(at_column, named_row[:, None], 0), axis=0)
        lane = columns[:LANES]
        names = jnp.where(lane < block - 1, names, jnp.where(lane == block - 1, own_rounds, 0))
        names = jnp.pad(names.astype(jnp.float32), (0, width - LANES))
        rows_out = jnp.dot(chosen.astype(jnp.bfloat16), flat_x, preferred_element_type=jnp.float32)
        last = (jnp.arange(block) == block - 1)[:, None]
        return jnp.where(last, names[None, :], rows_out).astype(jnp.bfloat16)

    def swap(values, step):
        return lax.ppermute(
            values, "hst", [(i, (i + step) % host_count) for i in range(host_count)]
        )

    def exchange(values):
        split = values.reshape(host_count, -1, values.shape[-1])
        split = lax.all_to_all(split, "hst", split_axis=0, concat_axis=0, tiled=True)
        return split.reshape(values.shape)

    def fold(values):
        parts = [values[:, i : i + folded] for i in range(0, spots, folded)]
        total = parts[0]
        for part in parts[1:]:
            total = total + part
        return total

    def adapt(inputs, names):
        mask = names[:, None] == spot_adapter[None, :]
        partial = lax.dot_general(
            inputs, flat_a, (((1,), (1,)), ((), ())), preferred_element_type=jnp.float32
        )
        partial = fold(jnp.where(mask, partial, 0.0))
        total = partial
        for hop in range(1, shares):
            total = total + lax.ppermute(
                partial, "mp", [(i, (i + hop) % shares) for i in range(shares)]
            )
        shrink = jnp.tile(total.astype(jnp.bfloat16), (1, spots // folded))
        spread = jnp.where(mask, shrink, 0)
        return jnp.dot(spread, flat_b, preferred_element_type=jnp.float32)

    def serve(received, block):
        names = received.reshape(-1, block, width)[:, block - 1, :LANES].astype(jnp.int32)
        rounds = jnp.max(names[:, block - 1])
        names = jnp.where(jnp.arange(block)[None, :] < block - 1, names[:, :block], 0)
        return adapt(received, names.reshape(-1)).astype(jnp.bfloat16), rounds

    def back(member, start, block, returned):
        return lax.dot_general(
            place(member, start, block).astype(jnp.bfloat16),
            returned,
            (((0,), (0,)), ((), ())),
            preferred_element_type=jnp.float32,
        )

    def one_round(start, block, base):
        if not by_shift:
            packed = jnp.concatenate([pack(member, start, block) for member in range(host_count)])
            adapted, rounds = serve(exchange(packed), block)
            returned = exchange(adapted).reshape(host_count, block, width)
            for member in range(host_count):
                base = base + back(member, start, block, returned[member])
            return base.astype(jnp.bfloat16), jnp.maximum(rounds, own_rounds)
        order = sorted(range(1, host_count), key=lambda s: min(s, host_count - s))
        received = {s: swap(pack(s, start, block), s) for s in order}
        rounds = own_rounds
        returned = {}
        for s in order:
            adapted, theirs = serve(received[s], block)
            rounds = jnp.maximum(rounds, theirs)
            returned[s] = swap(adapted, host_count - s)
        for s in order:
            base = (base + back(s, start, block, returned[s])).astype(jnp.bfloat16)
        return base, rounds

    own = adapt(flat_x, jnp.where(ahead == 0, named_row, 0)).astype(jnp.bfloat16)
    result, rounds = one_round(0, first_block, own)
    rounds = jnp.full((1, LANES), rounds, jnp.int32)
    for axis in ("rep", "groups"):
        size = lax.axis_size(axis)
        most = rounds
        for hop in range(1, size):
            most = jnp.maximum(
                most, lax.ppermute(rounds, axis, [(i, (i + hop) % size) for i in range(size)])
            )
        rounds = most

    def more(state):
        number, so_far = state
        start = first_block - 1 + number * (more_block - 1)
        so_far, _ = one_round(start, more_block, so_far)
        return number + 1, so_far

    _, result = lax.while_loop(
        lambda state: state[0] < rounds[0, 0], more, (jnp.int32(0), result)
    )
    return result.reshape(steps, step_rows, width)


def solution(mesh):
    return jax.shard_map(
        local,
        mesh=mesh,
        in_specs=(
            P(None, ("groups", "hst", "rep"), "mp"),
            P("hst", None, "mp"),
            P("hst", None, "mp"),
            P("groups"),
            P("groups"),
            P(None, ("groups", "hst", "rep"), None),
            P(None, ("groups", "hst", "rep")),
        ),
        out_specs=P(None, ("groups", "hst", "rep"), "mp"),
        check_vma=False,
    )
```

```python
import jax
import jax.numpy as jnp
from jax import lax
from jax.sharding import PartitionSpec as P

MOST_SHIFTS = 8
LANES = 128


def round_up(value, unit):
    return unit * -(-value // unit)


def local(
    activations,
    shrink_weight,
    expand_weight,
    former_layout_list,
    host_layout_list,
    target_host,
    target_position,
):
    host_count = lax.axis_size("hst")
    shares = lax.axis_size("mp")
    me = lax.axis_index("hst")
    local_adapters, rank_extent, width = shrink_weight.shape
    steps, step_rows, _ = activations.shape
    rows = steps * step_rows
    spots = local_adapters * rank_extent
    folded = LANES if spots % LANES == 0 and LANES % rank_extent == 0 else spots
    table_size = former_layout_list.shape[0]
    by_shift = host_count <= MOST_SHIFTS
    first_block = round_up(11 * rows // (8 * host_count), 8)
    more_block = min(first_block, 16)

    flat_x = activations.reshape(rows, width)
    flat_a = shrink_weight.reshape(spots, width)
    flat_b = expand_weight.reshape(spots, width)

    table = jnp.arange(table_size, dtype=jnp.int32)
    source = jnp.sum(
        jnp.where(host_layout_list[:, None] == former_layout_list[None, :], table[None, :], 0),
        axis=1,
    )
    wanted = (target_host[:, :, 0] * local_adapters + target_position).reshape(rows)
    served = jnp.sum(jnp.where(wanted[:, None] == table[None, :], source[None, :], 0), axis=1)
    owner = served // local_adapters
    named_row = served % local_adapters + 1
    ahead = lax.rem(owner - me + host_count, host_count)
    key = ahead if by_shift else jnp.where(ahead == 0, host_count, owner)

    hosts = jnp.arange(host_count, dtype=jnp.int32)
    in_block = key[:, None] == hosts[None, :]
    row_ids = jnp.arange(rows, dtype=jnp.int32)
    earlier = (row_ids[None, :] < row_ids[:, None]).astype(jnp.bfloat16)
    before = jnp.dot(
        earlier, in_block.astype(jnp.bfloat16), preferred_element_type=jnp.float32
    ).astype(jnp.int32)
    row_rank = jnp.sum(jnp.where(in_block, before, 0), axis=1)
    left = jnp.max(jnp.where(ahead == 0, 0, row_rank + 1)) - (first_block - 1)
    own_rounds = jnp.maximum(0, (left + more_block - 2) // (more_block - 1))

    columns = jnp.arange(width, dtype=jnp.int32)
    spot_adapter = jnp.arange(spots, dtype=jnp.int32) // rank_extent + 1

    def place(member, start, block):
        slot = jnp.arange(block, dtype=jnp.int32)[:, None]
        chosen = (
            (key[None, :] == member)
            & (slot + start == row_rank[None, :])
            & (slot < block - 1)
        )
        return chosen

    def pack(member, start, block):
        chosen = place(member, start, block)
        at_column = (key[:, None] == member) & (row_rank[:, None] == columns[None, :LANES] + start)
        names = jnp.sum(jnp.where(at_column, named_row[:, None], 0), axis=0)
        lane = columns[:LANES]
        names = jnp.where(lane < block - 1, names, jnp.where(lane == block - 1, own_rounds, 0))
        names = jnp.pad(names.astype(jnp.float32), (0, width - LANES))
        rows_out = jnp.dot(chosen.astype(jnp.bfloat16), flat_x, preferred_element_type=jnp.float32)
        last = (jnp.arange(block) == block - 1)[:, None]
        return jnp.where(last, names[None, :], rows_out).astype(jnp.bfloat16)

    def swap(values, step):
        return lax.ppermute(
            values, "hst", [(i, (i + step) % host_count) for i in range(host_count)]
        )

    def exchange(values):
        split = values.reshape(host_count, -1, values.shape[-1])
        split = lax.all_to_all(split, "hst", split_axis=0, concat_axis=0, tiled=True)
        return split.reshape(values.shape)

    def fold(values):
        parts = [values[:, i : i + folded] for i in range(0, spots, folded)]
        total = parts[0]
        for part in parts[1:]:
            total = total + part
        return total

    def adapt(inputs, names):
        mask = names[:, None] == spot_adapter[None, :]
        partial = lax.dot_general(
            inputs, flat_a, (((1,), (1,)), ((), ())), preferred_element_type=jnp.float32
        )
        partial = fold(jnp.where(mask, partial, 0.0))
        total = partial
        for hop in range(1, shares):
            total = total + lax.ppermute(
                partial, "mp", [(i, (i + hop) % shares) for i in range(shares)]
            )
        shrink = jnp.tile(total.astype(jnp.bfloat16), (1, spots // folded))
        spread = jnp.where(mask, shrink, 0)
        return jnp.dot(spread, flat_b, preferred_element_type=jnp.float32)

    def serve(received, block):
        names = received.reshape(-1, block, width)[:, block - 1, :LANES].astype(jnp.int32)
        rounds = jnp.max(names[:, block - 1])
        names = jnp.where(jnp.arange(block)[None, :] < block - 1, names[:, :block], 0)
        return adapt(received, names.reshape(-1)).astype(jnp.bfloat16), rounds

    def back(member, start, block, returned):
        return lax.dot_general(
            place(member, start, block).astype(jnp.bfloat16),
            returned,
            (((0,), (0,)), ((), ())),
            preferred_element_type=jnp.float32,
        )

    def one_round(start, block, base):
        if not by_shift:
            packed = jnp.concatenate([pack(member, start, block) for member in range(host_count)])
            adapted, rounds = serve(exchange(packed), block)
            returned = exchange(adapted).reshape(host_count, block, width)
            for member in range(host_count):
                base = base + back(member, start, block, returned[member])
            return base.astype(jnp.bfloat16), jnp.maximum(rounds, own_rounds)
        early = [s for s in range(1, host_count) if 2 * min(s, host_count - s) < host_count]
        late = [s for s in range(1, host_count) if s not in early]
        packed = {s: pack(s, start, block) for s in early + late}
        received = {s: swap(packed[s], s) for s in early}
        *held, base = lax.optimization_barrier(tuple(packed[s] for s in late) + (base,))
        packed = dict(zip(late, held))
        received.update({s: swap(packed[s], s) for s in late})
        rounds = own_rounds
        returned = {}
        for group in (early, late):
            adapted = {}
            for s in group:
                adapted[s], theirs = serve(received[s], block)
                rounds = jnp.maximum(rounds, theirs)
            if group is early:
                held = lax.optimization_barrier(
                    tuple(adapted[s] for s in early) + tuple(received[s] for s in late)
                )
                received.update(zip(late, held[len(early) :]))
            for s in group:
                returned[s] = swap(adapted[s], host_count - s)
        for s in early + late:
            base = (base + back(s, start, block, returned[s])).astype(jnp.bfloat16)
        return base, rounds

    own = adapt(flat_x, jnp.where(ahead == 0, named_row, 0)).astype(jnp.bfloat16)
    result, rounds = one_round(0, first_block, own)
    rounds = jnp.full((1, LANES), rounds, jnp.int32)
    for axis in ("rep", "groups"):
        size = lax.axis_size(axis)
        most = rounds
        for hop in range(1, size):
            most = jnp.maximum(
                most, lax.ppermute(rounds, axis, [(i, (i + hop) % size) for i in range(size)])
            )
        rounds = most

    def more(state):
        number, so_far = state
        start = first_block - 1 + number * (more_block - 1)
        so_far, _ = one_round(start, more_block, so_far)
        return number + 1, so_far

    _, result = lax.while_loop(
        lambda state: state[0] < rounds[0, 0], more, (jnp.int32(0), result)
    )
    return result.reshape(steps, step_rows, width)


def solution(mesh):
    return jax.shard_map(
        local,
        mesh=mesh,
        in_specs=(
            P(None, ("groups", "hst", "rep"), "mp"),
            P("hst", None, "mp"),
            P("hst", None, "mp"),
            P("groups"),
            P("groups"),
            P(None, ("groups", "hst", "rep"), None),
            P(None, ("groups", "hst", "rep")),
        ),
        out_specs=P(None, ("groups", "hst", "rep"), "mp"),
        check_vma=False,
    )
```

```python
import functools

import jax
import jax.numpy as jnp
from jax import lax
from jax.experimental import pallas as pl
from jax.experimental.pallas import tpu as pltpu
from jax.sharding import PartitionSpec as P

MOST_PAIRED = 8
LANES = 128
VMEM_BYTES = 32 << 20


def round_up(value, unit):
    return unit * -(-value // unit)


def block_names(block):
    count = block.shape[0]
    lane = lax.broadcasted_iota(jnp.int32, (count, LANES), 1)
    row = lax.broadcasted_iota(jnp.int32, (count, LANES), 0)
    last = block[count - 1 :, :LANES].astype(jnp.float32)
    return jnp.sum(
        jnp.where((lane == row) & (row < count - 1), last, 0.0), axis=1, keepdims=True
    )


def lane_adapter(first, rank_extent):
    lane = lax.broadcasted_iota(jnp.int32, (1, LANES), 1)
    return (first + lane // rank_extent + 1).astype(jnp.float32)


def shrink_kernel(counts, own, pieces, rank_extent, first_ref, *refs):
    blocks, refs = refs[: len(counts)], refs[len(counts) :]
    own_names = None
    if own:
        own_names, refs = refs[0], refs[1:]
    weights, (partial_ref, names_ref) = refs[:pieces], refs[pieces:]
    offset = 0
    for index, count in enumerate(counts):
        rows = blocks[index][...]
        names = own_names[...] if own and index == 0 else block_names(rows)
        total = jnp.zeros((count, LANES), jnp.float32)
        number = 0
        for weight in weights:
            for start in range(0, weight.shape[0], LANES):
                product = lax.dot_general(
                    rows,
                    weight[start : start + LANES, :],
                    (((1,), (1,)), ((), ())),
                    preferred_element_type=jnp.float32,
                )
                here = names == lane_adapter(first_ref[number], rank_extent)
                total = total + jnp.where(here, product, 0.0)
                number += 1
        partial_ref[offset : offset + count, :] = total
        names_ref[offset : offset + count, :] = jnp.broadcast_to(names, (count, LANES))
        offset += count


def expand_kernel(counts, shares, pieces, rank_extent, told, first_ref, *refs):
    if told:
        told_ref, refs = refs[0], refs[1:]
    partials, refs = refs[:shares], refs[shares:]
    names_ref, refs = refs[0], refs[1:]
    weights, refs = refs[:pieces], refs[pieces:]
    outs, spread_ref = refs[:-1], refs[-1]

    @pl.when(pl.program_id(0) == 0)
    def _():
        total = partials[0][...]
        for partial in partials[1:]:
            total = total + partial[...]
        shrink = total.astype(jnp.bfloat16).astype(jnp.float32)
        for number in range(spread_ref.shape[1] // LANES):
            here = names_ref[...] == lane_adapter(first_ref[number], rank_extent)
            spread_ref[:, number * LANES : (number + 1) * LANES] = jnp.where(
                here, shrink, 0.0
            ).astype(jnp.bfloat16)

    total = None
    column = 0
    for weight in weights:
        depth = weight.shape[0]
        product = jnp.dot(
            spread_ref[:, column : column + depth],
            weight[...],
            preferred_element_type=jnp.float32,
        )
        total = product if total is None else total + product
        column += depth
    offset = 0
    for count, out in zip(counts, outs):
        values = total[offset : offset + count, :]
        if told:
            row = lax.broadcasted_iota(jnp.int32, values.shape, 0)
            values = jnp.where(row == count - 1, told_ref[0].astype(jnp.float32), values)
        out[...] = values.astype(out.dtype)
        offset += count


def back_kernel(blocks, base_ref, *refs):
    places, returned, outs = refs[:blocks], refs[blocks : 2 * blocks], refs[2 * blocks :]
    out_ref = outs[0]
    total = base_ref[...].astype(jnp.float32)
    for place, block in zip(places, returned):
        total = total + jnp.dot(place[...], block[...], preferred_element_type=jnp.float32)
    out_ref[...] = total.astype(out_ref.dtype)
    if len(outs) == 1:
        return

    @pl.when(pl.program_id(0) == 0)
    def _():
        told = jnp.float32(0)
        for block in returned:
            rows = block[...]
            told = jnp.maximum(told, jnp.max(rows[rows.shape[0] - 1 :, :LANES].astype(jnp.float32)))
        outs[1][0] = told.astype(jnp.int32)


def shrink_call(blocks, own_names, weights, firsts, rank_extent):
    counts = [block.shape[0] for block in blocks]
    rows = sum(counts)
    width = blocks[0].shape[1]
    spots = sum(weight.shape[0] for weight in weights)
    names = [] if own_names is None else [own_names]
    whole = pl.BlockSpec(memory_space=pltpu.VMEM)
    return pl.pallas_call(
        functools.partial(
            shrink_kernel, counts, own_names is not None, len(weights), rank_extent
        ),
        out_shape=(jax.ShapeDtypeStruct((rows, LANES), jnp.float32),) * 2,
        in_specs=[pl.BlockSpec(memory_space=pltpu.SMEM)]
        + [whole] * (len(blocks) + len(names) + len(weights)),
        out_specs=(whole, whole),
        compiler_params=pltpu.CompilerParams(vmem_limit_bytes=VMEM_BYTES),
        cost_estimate=pl.CostEstimate(
            flops=2 * rows * spots * width,
            bytes_accessed=2 * (rows + spots) * width,
            transcendentals=0,
        ),
    )(firsts, *blocks, *names, *weights)


def back_call(base, places, returned, told, weight=1):
    rows, width = base.shape
    tile = width // 6 if width % (6 * LANES) == 0 else width
    tiles = lambda count: pl.BlockSpec((count, tile), lambda i: (0, i))
    return pl.pallas_call(
        functools.partial(back_kernel, len(returned)),
        grid=(width // tile,),
        out_shape=[jax.ShapeDtypeStruct((rows, width), jnp.bfloat16)]
        + [jax.ShapeDtypeStruct((1,), jnp.int32)] * told,
        in_specs=[tiles(rows)]
        + [pl.BlockSpec(place.shape, lambda i: (0, 0)) for place in places]
        + [tiles(block.shape[0]) for block in returned],
        out_specs=[tiles(rows)] + [pl.BlockSpec(memory_space=pltpu.SMEM)] * told,
        compiler_params=pltpu.CompilerParams(vmem_limit_bytes=VMEM_BYTES),
        cost_estimate=pl.CostEstimate(
            flops=2 * weight * rows * width * sum(block.shape[0] for block in returned),
            bytes_accessed=4 * weight * rows * width,
            transcendentals=0,
        ),
    )(base, *places, *returned)


def expand_call(partials, names, weights, firsts, counts, rank_extent, told=None):
    width = weights[0].shape[1]
    rows = names.shape[0]
    spots = sum(weight.shape[0] for weight in weights)
    tile = width // 6 if width % (6 * LANES) == 0 else width
    whole = pl.BlockSpec(memory_space=pltpu.VMEM)
    return pl.pallas_call(
        functools.partial(
            expand_kernel, counts, len(partials), len(weights), rank_extent, told is not None
        ),
        grid=(width // tile,),
        out_shape=[jax.ShapeDtypeStruct((count, width), jnp.bfloat16) for count in counts],
        in_specs=[pl.BlockSpec(memory_space=pltpu.SMEM)] * (1 if told is None else 2)
        + [whole] * (len(partials) + 1)
        + [pl.BlockSpec((weight.shape[0], tile), lambda i: (0, i)) for weight in weights],
        out_specs=[pl.BlockSpec((count, tile), lambda i: (0, i)) for count in counts],
        scratch_shapes=[pltpu.VMEM((rows, spots), jnp.bfloat16)],
        compiler_params=pltpu.CompilerParams(vmem_limit_bytes=VMEM_BYTES),
        cost_estimate=pl.CostEstimate(
            flops=2 * rows * spots * width,
            bytes_accessed=2 * (rows + spots) * width,
            transcendentals=0,
        ),
    )(firsts, *([] if told is None else [told]), *partials, names, *weights)


def local(
    activations,
    shrink_weight,
    expand_weight,
    former_layout_list,
    host_layout_list,
    target_host,
    target_position,
):
    host_count = lax.axis_size("hst")
    shares = lax.axis_size("mp")
    me = lax.axis_index("hst")
    local_adapters, rank_extent, width = shrink_weight.shape
    steps, step_rows, _ = activations.shape
    rows = steps * step_rows
    spots = local_adapters * rank_extent
    folded = LANES if spots % LANES == 0 and LANES % rank_extent == 0 else spots
    table_size = former_layout_list.shape[0]
    paired = host_count <= MOST_PAIRED and host_count & (host_count - 1) == 0
    first_block = round_up(11 * rows // (8 * host_count), 8)
    more_block = min(first_block, 16)

    flat_x = activations.reshape(rows, width)
    flat_a = shrink_weight.reshape(spots, width)
    flat_b = expand_weight.reshape(spots, width)

    table = jnp.arange(table_size, dtype=jnp.int32)
    source = jnp.sum(
        jnp.where(host_layout_list[:, None] == former_layout_list[None, :], table[None, :], 0),
        axis=1,
    )
    wanted = (target_host[:, :, 0] * local_adapters + target_position).reshape(rows)
    served = jnp.sum(jnp.where(wanted[:, None] == table[None, :], source[None, :], 0), axis=1)
    owner = served // local_adapters
    named_row = served % local_adapters + 1
    stays = owner == me
    key = owner ^ me if paired else jnp.where(stays, host_count, owner)

    hosts = jnp.arange(host_count, dtype=jnp.int32)
    in_block = key[:, None] == hosts[None, :]
    row_ids = jnp.arange(rows, dtype=jnp.int32)
    earlier = (row_ids[None, :] < row_ids[:, None]).astype(jnp.bfloat16)
    before = jnp.dot(
        earlier, in_block.astype(jnp.bfloat16), preferred_element_type=jnp.float32
    ).astype(jnp.int32)
    row_rank = jnp.sum(jnp.where(in_block, before, 0), axis=1)
    left = jnp.max(jnp.where(stays, 0, row_rank + 1)) - (first_block - 1)
    own_rounds = jnp.maximum(0, (left + more_block - 2) // (more_block - 1))

    columns = jnp.arange(width, dtype=jnp.int32)
    spot_adapter = jnp.arange(spots, dtype=jnp.int32) // rank_extent + 1

    def place(member, start, block, key, row_rank):
        slot = jnp.arange(block, dtype=jnp.int32)[:, None]
        chosen = (
            (key[None, :] == member)
            & (slot + start == row_rank[None, :])
            & (slot < block - 1)
        )
        return chosen.astype(jnp.bfloat16)

    def pack(member, start, block, key, row_rank, told):
        at_column = (key[:, None] == member) & (row_rank[:, None] == columns[None, :LANES] + start)
        names = jnp.sum(jnp.where(at_column, named_row[:, None], 0), axis=0)
        lane = columns[:LANES]
        names = jnp.where(lane < block - 1, names, jnp.where(lane == block - 1, told, 0))
        names = jnp.pad(names.astype(jnp.float32), (0, width - LANES))
        rows_out = jnp.dot(
            place(member, start, block, key, row_rank),
            flat_x,
            preferred_element_type=jnp.float32,
        )
        last = (jnp.arange(block) == block - 1)[:, None]
        return jnp.where(last, names[None, :], rows_out).astype(jnp.bfloat16)

    def swap(values, step):
        return lax.ppermute(values, "hst", [(i, i ^ step) for i in range(host_count)])

    def exchange(values):
        split = values.reshape(host_count, -1, values.shape[-1])
        split = lax.all_to_all(split, "hst", split_axis=0, concat_axis=0, tiled=True)
        return split.reshape(values.shape)

    def fold(values):
        parts = [values[:, i : i + folded] for i in range(0, spots, folded)]
        total = parts[0]
        for part in parts[1:]:
            total = total + part
        return total

    def adapt(inputs, names):
        mask = names[:, None] == spot_adapter[None, :]
        partial = lax.dot_general(
            inputs, flat_a, (((1,), (1,)), ((), ())), preferred_element_type=jnp.float32
        )
        partial = fold(jnp.where(mask, partial, 0.0))
        total = partial
        for hop in range(1, shares):
            total = total + lax.ppermute(
                partial, "mp", [(i, (i + hop) % shares) for i in range(shares)]
            )
        shrink = jnp.tile(total.astype(jnp.bfloat16), (1, spots // folded))
        spread = jnp.where(mask, shrink, 0)
        return jnp.dot(spread, flat_b, preferred_element_type=jnp.float32)

    def serve(received, block):
        names = received.reshape(-1, block, width)[:, block - 1, :LANES].astype(jnp.int32)
        rounds = jnp.max(names[:, block - 1])
        names = jnp.where(jnp.arange(block)[None, :] < block - 1, names[:, :block], 0)
        return adapt(received, names.reshape(-1)).astype(jnp.bfloat16), rounds

    def back(member, start, block, returned):
        return lax.dot_general(
            place(member, start, block, key, row_rank),
            returned,
            (((0,), (0,)), ((), ())),
            preferred_element_type=jnp.float32,
        )

    def one_round(start, block, base):
        if not paired:
            packed = jnp.concatenate([pack(member, start, block, key, row_rank, own_rounds) for member in range(host_count)])
            adapted, rounds = serve(exchange(packed), block)
            returned = exchange(adapted).reshape(host_count, block, width)
            for member in range(host_count):
                base = base + back(member, start, block, returned[member])
            return base.astype(jnp.bfloat16), jnp.maximum(rounds, own_rounds)
        received = {s: swap(pack(s, start, block, key, row_rank, own_rounds), s) for s in range(1, host_count)}
        rounds = own_rounds
        for s in range(1, host_count):
            adapted, theirs = serve(received[s], block)
            rounds = jnp.maximum(rounds, theirs)
            returned = swap(adapted, s)
            base = (base + back(s, start, block, returned)).astype(jnp.bfloat16)
        return base, rounds

    def agree(rounds):
        rounds = jnp.full((1, LANES), rounds, jnp.int32)
        for axis in ("rep", "groups"):
            size = lax.axis_size(axis)
            most = rounds
            for hop in range(1, size):
                most = jnp.maximum(
                    most,
                    lax.ppermute(rounds, axis, [(i, (i + hop) % size) for i in range(size)]),
                )
            rounds = most
        return rounds

    def over_shares(partial):
        return [partial] + [
            lax.ppermute(partial, "mp", [(i, (i + hop) % shares) for i in range(shares)])
            for hop in range(1, shares)
        ]

    def paired_round(key, row_rank):
        firsts = (LANES // rank_extent) * jnp.arange(spots // LANES, dtype=jnp.int32)
        block = first_block

        def shrink(blocks, names):
            return shrink_call(blocks, names, [flat_a], firsts, rank_extent)

        def expand(blocks, partial, names, told=None):
            return expand_call(
                over_shares(partial),
                names,
                [flat_b],
                firsts,
                [rows_in.shape[0] for rows_in in blocks],
                rank_extent,
                told,
            )

        near = list(range(1, host_count // 2))
        far = list(range(host_count // 2, host_count))
        order = near + far
        order = far[:1] + near + far[1:]
        first, last = far[0], far[-1]
        packed = pack(first, 0, block, key, row_rank, 0)
        received = {first: swap(packed, first)}
        own_names = jnp.where(stays, named_row, 0).astype(jnp.float32)[:, None]
        own_names, rounds, _ = lax.optimization_barrier((own_names, own_rounds, packed))
        rounds = agree(rounds)[0]
        partial, names = shrink([flat_x], own_names)
        partial, key, row_rank = lax.optimization_barrier((partial, key, row_rank))
        for s in near + far[1:-1]:
            received[s] = swap(pack(s, 0, block, key, row_rank, 0), s)
        packed = pack(last, 0, block, key, row_rank, rounds[0])
        (base,) = expand([flat_x], partial, names)
        base, packed = lax.optimization_barrier((base, packed))
        received[last] = swap(packed, last)
        returned = {}
        for number, s in enumerate(order):
            told = None if s == last else rounds
            (adapted,) = expand([received[s]], *shrink([received[s]], None), told)
            if s != last:
                later = order[number + 1]
                _, received[later] = lax.optimization_barrier((adapted, received[later]))
            returned[s] = swap(adapted, s)
        places = {s: place(s, 0, block, key, row_rank).T for s in order}
        early = order[:-1]
        base, told = back_call(
            base, [places[s] for s in early], [returned[s] for s in early], True, 30
        )
        result = jnp.dot(places[last], returned[last], preferred_element_type=jnp.float32)
        result = (result + base).astype(jnp.bfloat16)
        told = jnp.maximum(told[0], received[last][block - 1, block - 1].astype(jnp.int32))
        return result, jnp.maximum(told, rounds[0])

    if paired and spots % LANES == 0 and LANES % rank_extent == 0:
        result, rounds = paired_round(key, row_rank)
    else:
        own = adapt(flat_x, jnp.where(stays, named_row, 0)).astype(jnp.bfloat16)
        result, rounds = one_round(0, first_block, own)
        rounds = agree(rounds)[0, 0]
    def more(state):
        number, so_far = state
        start = first_block - 1 + number * (more_block - 1)
        so_far, _ = one_round(start, more_block, so_far)
        return number + 1, so_far

    _, result = lax.while_loop(
        lambda state: state[0] < rounds, more, (jnp.int32(0), result)
    )
    return result.reshape(steps, step_rows, width)


def solution(mesh):
    return jax.shard_map(
        local,
        mesh=mesh,
        in_specs=(
            P(None, ("groups", "hst", "rep"), "mp"),
            P("hst", None, "mp"),
            P("hst", None, "mp"),
            P("groups"),
            P("groups"),
            P(None, ("groups", "hst", "rep"), None),
            P(None, ("groups", "hst", "rep")),
        ),
        out_specs=P(None, ("groups", "hst", "rep"), "mp"),
        check_vma=False,
    )
```

```python
import functools

import jax
import jax.numpy as jnp
from jax import lax
from jax.experimental import pallas as pl
from jax.experimental.pallas import tpu as pltpu
from jax.sharding import PartitionSpec as P

MOST_PAIRED = 8
LANES = 128
VMEM_BYTES = 32 << 20


def round_up(value, unit):
    return unit * -(-value // unit)


def block_names(block):
    count = block.shape[0]
    lane = lax.broadcasted_iota(jnp.int32, (count, LANES), 1)
    row = lax.broadcasted_iota(jnp.int32, (count, LANES), 0)
    last = block[count - 1 :, :LANES].astype(jnp.float32)
    return jnp.sum(
        jnp.where((lane == row) & (row < count - 1), last, 0.0), axis=1, keepdims=True
    )


def lane_adapter(first, rank_extent):
    lane = lax.broadcasted_iota(jnp.int32, (1, LANES), 1)
    return (first + lane // rank_extent + 1).astype(jnp.float32)


def shrink_kernel(counts, own, pieces, rank_extent, first_ref, *refs):
    blocks, refs = refs[: len(counts)], refs[len(counts) :]
    own_names = None
    if own:
        own_names, refs = refs[0], refs[1:]
    weights, (partial_ref, names_ref) = refs[:pieces], refs[pieces:]
    offset = 0
    for index, count in enumerate(counts):
        rows = blocks[index][...]
        names = own_names[...] if own and index == 0 else block_names(rows)
        total = jnp.zeros((count, LANES), jnp.float32)
        number = 0
        for weight in weights:
            for start in range(0, weight.shape[0], LANES):
                product = lax.dot_general(
                    rows,
                    weight[start : start + LANES, :],
                    (((1,), (1,)), ((), ())),
                    preferred_element_type=jnp.float32,
                )
                here = names == lane_adapter(first_ref[number], rank_extent)
                total = total + jnp.where(here, product, 0.0)
                number += 1
        partial_ref[offset : offset + count, :] = total
        names_ref[offset : offset + count, :] = jnp.broadcast_to(names, (count, LANES))
        offset += count


def expand_kernel(counts, shares, pieces, rank_extent, told, first_ref, *refs):
    if told:
        told_ref, refs = refs[0], refs[1:]
    partials, refs = refs[:shares], refs[shares:]
    names_ref, refs = refs[0], refs[1:]
    weights, refs = refs[:pieces], refs[pieces:]
    outs, spread_ref = refs[:-1], refs[-1]

    @pl.when(pl.program_id(0) == 0)
    def _():
        total = partials[0][...]
        for partial in partials[1:]:
            total = total + partial[...]
        shrink = total.astype(jnp.bfloat16).astype(jnp.float32)
        for number in range(spread_ref.shape[1] // LANES):
            here = names_ref[...] == lane_adapter(first_ref[number], rank_extent)
            spread_ref[:, number * LANES : (number + 1) * LANES] = jnp.where(
                here, shrink, 0.0
            ).astype(jnp.bfloat16)

    total = None
    column = 0
    for weight in weights:
        depth = weight.shape[0]
        product = jnp.dot(
            spread_ref[:, column : column + depth],
            weight[...],
            preferred_element_type=jnp.float32,
        )
        total = product if total is None else total + product
        column += depth
    offset = 0
    for count, out in zip(counts, outs):
        values = total[offset : offset + count, :]
        if told:
            row = lax.broadcasted_iota(jnp.int32, values.shape, 0)
            values = jnp.where(row == count - 1, told_ref[0].astype(jnp.float32), values)
        out[...] = values.astype(out.dtype)
        offset += count


def route_kernel(
    block, member, local_adapters, me_ref, source_ref, wanted_ref, x_ref, packed_ref, route_ref, most_ref
):
    table = source_ref.shape[1]
    rows = x_ref.shape[0]
    down = lax.broadcasted_iota(jnp.int32, (table, table), 0)
    across = lax.broadcasted_iota(jnp.int32, (table, table), 1)
    source = jnp.sum(jnp.where(down == across, source_ref[...], 0), axis=1, keepdims=True)
    wanted = wanted_ref[...]
    entry = lax.broadcasted_iota(jnp.int32, (table, rows), 0)
    served = jnp.sum(jnp.where(entry == wanted, source, 0), axis=0, keepdims=True)
    owner = lax.div(served, jnp.int32(local_adapters))
    name = served - owner * local_adapters + 1
    key = owner ^ me_ref[0]
    member_of = lax.broadcasted_iota(jnp.int32, (8, rows), 0) == key
    earlier = lax.broadcasted_iota(jnp.int32, (rows, rows), 0) < lax.broadcasted_iota(
        jnp.int32, (rows, rows), 1
    )
    before = jnp.dot(
        member_of.astype(jnp.bfloat16),
        earlier.astype(jnp.bfloat16),
        preferred_element_type=jnp.float32,
    ).astype(jnp.int32)
    rank = jnp.sum(jnp.where(member_of, before, 0), axis=0, keepdims=True)
    most_ref[0] = jnp.max(jnp.where(key == 0, 0, rank + 1))
    line = lax.broadcasted_iota(jnp.int32, (8, rows), 0)
    route_ref[...] = jnp.where(line == 0, key, jnp.where(line == 1, rank, name))

    slot = lax.broadcasted_iota(jnp.int32, (block, rows), 0)
    chosen = (key == member) & (slot == rank) & (slot < block - 1)
    names = jnp.sum(jnp.where(chosen, name, 0), axis=1, keepdims=True)
    turn = lax.broadcasted_iota(jnp.int32, (block, LANES), 0) == lax.broadcasted_iota(
        jnp.int32, (block, LANES), 1
    )
    names = jnp.sum(jnp.where(turn, names, 0), axis=0, keepdims=True).astype(jnp.float32)
    packed = jnp.dot(
        chosen.astype(jnp.bfloat16), x_ref[...], preferred_element_type=jnp.float32
    )
    packed_ref[...] = packed.astype(packed_ref.dtype)
    last = lax.broadcasted_iota(jnp.int32, (block, LANES), 0) == block - 1
    packed_ref[:, :LANES] = jnp.where(last, names, packed[:, :LANES]).astype(packed_ref.dtype)


def route_call(me, source, wanted, flat_x, block, member, local_adapters):
    rows, width = flat_x.shape
    whole = pl.BlockSpec(memory_space=pltpu.VMEM)
    scalar = pl.BlockSpec(memory_space=pltpu.SMEM)
    return pl.pallas_call(
        functools.partial(route_kernel, block, member, local_adapters),
        out_shape=(
            jax.ShapeDtypeStruct((block, width), jnp.bfloat16),
            jax.ShapeDtypeStruct((8, rows), jnp.int32),
            jax.ShapeDtypeStruct((1,), jnp.int32),
        ),
        in_specs=[scalar, whole, whole, whole],
        out_specs=(whole, whole, scalar),
        compiler_params=pltpu.CompilerParams(vmem_limit_bytes=VMEM_BYTES),
    )(me.reshape(1), source.reshape(1, -1), wanted.reshape(1, -1), flat_x)


def back_kernel(blocks, base_ref, *refs):
    places, returned, outs = refs[:blocks], refs[blocks : 2 * blocks], refs[2 * blocks :]
    out_ref = outs[0]
    total = base_ref[...].astype(jnp.float32)
    for place, block in zip(places, returned):
        total = total + jnp.dot(place[...], block[...], preferred_element_type=jnp.float32)
    out_ref[...] = total.astype(out_ref.dtype)
    if len(outs) == 1:
        return

    @pl.when(pl.program_id(0) == 0)
    def _():
        told = jnp.float32(0)
        for block in returned:
            rows = block[...]
            told = jnp.maximum(told, jnp.max(rows[rows.shape[0] - 1 :, :LANES].astype(jnp.float32)))
        outs[1][0] = told.astype(jnp.int32)


def shrink_call(blocks, own_names, weights, firsts, rank_extent):
    counts = [block.shape[0] for block in blocks]
    rows = sum(counts)
    width = blocks[0].shape[1]
    spots = sum(weight.shape[0] for weight in weights)
    names = [] if own_names is None else [own_names]
    whole = pl.BlockSpec(memory_space=pltpu.VMEM)
    return pl.pallas_call(
        functools.partial(
            shrink_kernel, counts, own_names is not None, len(weights), rank_extent
        ),
        out_shape=(jax.ShapeDtypeStruct((rows, LANES), jnp.float32),) * 2,
        in_specs=[pl.BlockSpec(memory_space=pltpu.SMEM)]
        + [whole] * (len(blocks) + len(names) + len(weights)),
        out_specs=(whole, whole),
        compiler_params=pltpu.CompilerParams(vmem_limit_bytes=VMEM_BYTES),
        cost_estimate=pl.CostEstimate(
            flops=2 * rows * spots * width,
            bytes_accessed=2 * (rows + spots) * width,
            transcendentals=0,
        ),
    )(firsts, *blocks, *names, *weights)


def back_call(base, places, returned, told, weight=1):
    rows, width = base.shape
    tile = width // 6 if width % (6 * LANES) == 0 else width
    tiles = lambda count: pl.BlockSpec((count, tile), lambda i: (0, i))
    return pl.pallas_call(
        functools.partial(back_kernel, len(returned)),
        grid=(width // tile,),
        out_shape=[jax.ShapeDtypeStruct((rows, width), jnp.bfloat16)]
        + [jax.ShapeDtypeStruct((1,), jnp.int32)] * told,
        in_specs=[tiles(rows)]
        + [pl.BlockSpec(place.shape, lambda i: (0, 0)) for place in places]
        + [tiles(block.shape[0]) for block in returned],
        out_specs=[tiles(rows)] + [pl.BlockSpec(memory_space=pltpu.SMEM)] * told,
        compiler_params=pltpu.CompilerParams(vmem_limit_bytes=VMEM_BYTES),
        cost_estimate=pl.CostEstimate(
            flops=2 * weight * rows * width * sum(block.shape[0] for block in returned),
            bytes_accessed=4 * weight * rows * width,
            transcendentals=0,
        ),
    )(base, *places, *returned)


def expand_call(partials, names, weights, firsts, counts, rank_extent, told=None):
    width = weights[0].shape[1]
    rows = names.shape[0]
    spots = sum(weight.shape[0] for weight in weights)
    tile = width // 6 if width % (6 * LANES) == 0 else width
    whole = pl.BlockSpec(memory_space=pltpu.VMEM)
    return pl.pallas_call(
        functools.partial(
            expand_kernel, counts, len(partials), len(weights), rank_extent, told is not None
        ),
        grid=(width // tile,),
        out_shape=[jax.ShapeDtypeStruct((count, width), jnp.bfloat16) for count in counts],
        in_specs=[pl.BlockSpec(memory_space=pltpu.SMEM)] * (1 if told is None else 2)
        + [whole] * (len(partials) + 1)
        + [pl.BlockSpec((weight.shape[0], tile), lambda i: (0, i)) for weight in weights],
        out_specs=[pl.BlockSpec((count, tile), lambda i: (0, i)) for count in counts],
        scratch_shapes=[pltpu.VMEM((rows, spots), jnp.bfloat16)],
        compiler_params=pltpu.CompilerParams(vmem_limit_bytes=VMEM_BYTES),
        cost_estimate=pl.CostEstimate(
            flops=2 * rows * spots * width,
            bytes_accessed=2 * (rows + spots) * width,
            transcendentals=0,
        ),
    )(firsts, *([] if told is None else [told]), *partials, names, *weights)


def local(
    activations,
    shrink_weight,
    expand_weight,
    former_layout_list,
    host_layout_list,
    target_host,
    target_position,
):
    host_count = lax.axis_size("hst")
    shares = lax.axis_size("mp")
    me = lax.axis_index("hst")
    local_adapters, rank_extent, width = shrink_weight.shape
    steps, step_rows, _ = activations.shape
    rows = steps * step_rows
    spots = local_adapters * rank_extent
    folded = LANES if spots % LANES == 0 and LANES % rank_extent == 0 else spots
    table_size = former_layout_list.shape[0]
    paired = host_count <= MOST_PAIRED and host_count & (host_count - 1) == 0
    first_block = round_up(11 * rows // (8 * host_count), 8)
    more_block = min(first_block, 16)

    flat_x = activations.reshape(rows, width)
    flat_a = shrink_weight.reshape(spots, width)
    flat_b = expand_weight.reshape(spots, width)

    table = jnp.arange(table_size, dtype=jnp.int32)
    source = jnp.sum(
        jnp.where(host_layout_list[:, None] == former_layout_list[None, :], table[None, :], 0),
        axis=1,
    )
    wanted = (target_host[:, :, 0] * local_adapters + target_position).reshape(rows)

    def route():
        served = jnp.sum(jnp.where(wanted[:, None] == table[None, :], source[None, :], 0), axis=1)
        owner = served // local_adapters
        key = owner ^ me if paired else jnp.where(owner == me, host_count, owner)
        in_block = key[:, None] == jnp.arange(host_count, dtype=jnp.int32)[None, :]
        row_ids = jnp.arange(rows, dtype=jnp.int32)
        earlier = (row_ids[None, :] < row_ids[:, None]).astype(jnp.bfloat16)
        before = jnp.dot(
            earlier, in_block.astype(jnp.bfloat16), preferred_element_type=jnp.float32
        ).astype(jnp.int32)
        row_rank = jnp.sum(jnp.where(in_block, before, 0), axis=1)
        most = jnp.max(jnp.where(owner == me, 0, row_rank + 1))
        return key, row_rank, served % local_adapters + 1, owner == me, most

    tiled = paired and spots % LANES == 0 and LANES % rank_extent == 0
    if tiled:
        first_packed, lines, most = route_call(
            me, source, wanted, flat_x, first_block, host_count // 2, local_adapters
        )
        key, row_rank, named_row, most = lines[0], lines[1], lines[2], most[0]
        stays = key == 0
    else:
        key, row_rank, named_row, stays, most = route()
    left = most - (first_block - 1)
    own_rounds = jnp.maximum(0, (left + more_block - 2) // (more_block - 1))

    columns = jnp.arange(width, dtype=jnp.int32)
    spot_adapter = jnp.arange(spots, dtype=jnp.int32) // rank_extent + 1

    def place(member, start, block, key, row_rank):
        slot = jnp.arange(block, dtype=jnp.int32)[:, None]
        chosen = (
            (key[None, :] == member)
            & (slot + start == row_rank[None, :])
            & (slot < block - 1)
        )
        return chosen.astype(jnp.bfloat16)

    def pack(member, start, block, key, row_rank, told):
        at_column = (key[:, None] == member) & (row_rank[:, None] == columns[None, :LANES] + start)
        names = jnp.sum(jnp.where(at_column, named_row[:, None], 0), axis=0)
        lane = columns[:LANES]
        names = jnp.where(lane < block - 1, names, jnp.where(lane == block - 1, told, 0))
        names = jnp.pad(names.astype(jnp.float32), (0, width - LANES))
        rows_out = jnp.dot(
            place(member, start, block, key, row_rank),
            flat_x,
            preferred_element_type=jnp.float32,
        )
        last = (jnp.arange(block) == block - 1)[:, None]
        return jnp.where(last, names[None, :], rows_out).astype(jnp.bfloat16)

    def swap(values, step):
        return lax.ppermute(values, "hst", [(i, i ^ step) for i in range(host_count)])

    def exchange(values):
        split = values.reshape(host_count, -1, values.shape[-1])
        split = lax.all_to_all(split, "hst", split_axis=0, concat_axis=0, tiled=True)
        return split.reshape(values.shape)

    def fold(values):
        parts = [values[:, i : i + folded] for i in range(0, spots, folded)]
        total = parts[0]
        for part in parts[1:]:
            total = total + part
        return total

    def adapt(inputs, names):
        mask = names[:, None] == spot_adapter[None, :]
        partial = lax.dot_general(
            inputs, flat_a, (((1,), (1,)), ((), ())), preferred_element_type=jnp.float32
        )
        partial = fold(jnp.where(mask, partial, 0.0))
        total = partial
        for hop in range(1, shares):
            total = total + lax.ppermute(
                partial, "mp", [(i, (i + hop) % shares) for i in range(shares)]
            )
        shrink = jnp.tile(total.astype(jnp.bfloat16), (1, spots // folded))
        spread = jnp.where(mask, shrink, 0)
        return jnp.dot(spread, flat_b, preferred_element_type=jnp.float32)

    def serve(received, block):
        names = received.reshape(-1, block, width)[:, block - 1, :LANES].astype(jnp.int32)
        rounds = jnp.max(names[:, block - 1])
        names = jnp.where(jnp.arange(block)[None, :] < block - 1, names[:, :block], 0)
        return adapt(received, names.reshape(-1)).astype(jnp.bfloat16), rounds

    def back(member, start, block, returned):
        return lax.dot_general(
            place(member, start, block, key, row_rank),
            returned,
            (((0,), (0,)), ((), ())),
            preferred_element_type=jnp.float32,
        )

    def one_round(start, block, base):
        if not paired:
            packed = jnp.concatenate([pack(member, start, block, key, row_rank, own_rounds) for member in range(host_count)])
            adapted, rounds = serve(exchange(packed), block)
            returned = exchange(adapted).reshape(host_count, block, width)
            for member in range(host_count):
                base = base + back(member, start, block, returned[member])
            return base.astype(jnp.bfloat16), jnp.maximum(rounds, own_rounds)
        received = {s: swap(pack(s, start, block, key, row_rank, own_rounds), s) for s in range(1, host_count)}
        rounds = own_rounds
        for s in range(1, host_count):
            adapted, theirs = serve(received[s], block)
            rounds = jnp.maximum(rounds, theirs)
            returned = swap(adapted, s)
            base = (base + back(s, start, block, returned)).astype(jnp.bfloat16)
        return base, rounds

    def agree(rounds):
        rounds = jnp.full((1, LANES), rounds, jnp.int32)
        for axis in ("rep", "groups"):
            size = lax.axis_size(axis)
            most = rounds
            for hop in range(1, size):
                most = jnp.maximum(
                    most,
                    lax.ppermute(rounds, axis, [(i, (i + hop) % size) for i in range(size)]),
                )
            rounds = most
        return rounds

    def over_shares(partial):
        return [partial] + [
            lax.ppermute(partial, "mp", [(i, (i + hop) % shares) for i in range(shares)])
            for hop in range(1, shares)
        ]

    def paired_round(key, row_rank):
        firsts = (LANES // rank_extent) * jnp.arange(spots // LANES, dtype=jnp.int32)
        block = first_block

        def shrink(blocks, names):
            return shrink_call(blocks, names, [flat_a], firsts, rank_extent)

        def expand(blocks, partial, names, told=None):
            return expand_call(
                over_shares(partial),
                names,
                [flat_b],
                firsts,
                [rows_in.shape[0] for rows_in in blocks],
                rank_extent,
                told,
            )

        near = list(range(1, host_count // 2))
        far = list(range(host_count // 2, host_count))
        order = near + far
        order = far[:1] + near + far[1:]
        first, last = far[0], far[-1]
        packed = first_packed
        received = {first: swap(packed, first)}
        own_names = jnp.where(stays, named_row, 0).astype(jnp.float32)[:, None]
        own_names, rounds, _ = lax.optimization_barrier((own_names, own_rounds, packed))
        rounds = agree(rounds)[0]
        partial, names = shrink([flat_x], own_names)
        partial, key, row_rank = lax.optimization_barrier((partial, key, row_rank))
        for s in near + far[1:-1]:
            received[s] = swap(pack(s, 0, block, key, row_rank, 0), s)
        packed = pack(last, 0, block, key, row_rank, rounds[0])
        (base,) = expand([flat_x], partial, names)
        base, packed = lax.optimization_barrier((base, packed))
        received[last] = swap(packed, last)
        returned = {}
        for number, s in enumerate(order):
            told = None if s == last else rounds
            (adapted,) = expand([received[s]], *shrink([received[s]], None), told)
            if s != last:
                later = order[number + 1]
                _, received[later] = lax.optimization_barrier((adapted, received[later]))
            returned[s] = swap(adapted, s)
        places = {s: place(s, 0, block, key, row_rank).T for s in order}
        early = order[:-1]
        base, told = back_call(
            base, [places[s] for s in early], [returned[s] for s in early], True, 30
        )
        base, place_last = lax.optimization_barrier((base, places[last]))
        result = jnp.dot(place_last, returned[last], preferred_element_type=jnp.float32)
        result = (result + base).astype(jnp.bfloat16)
        told = jnp.maximum(told[0], received[last][block - 1, block - 1].astype(jnp.int32))
        return result, jnp.maximum(told, rounds[0])

    if tiled:
        result, rounds = paired_round(key, row_rank)
    else:
        own = adapt(flat_x, jnp.where(stays, named_row, 0)).astype(jnp.bfloat16)
        result, rounds = one_round(0, first_block, own)
        rounds = agree(rounds)[0, 0]
    def more(state):
        number, so_far = state
        start = first_block - 1 + number * (more_block - 1)
        so_far, _ = one_round(start, more_block, so_far)
        return number + 1, so_far

    _, result = lax.while_loop(
        lambda state: state[0] < rounds, more, (jnp.int32(0), result)
    )
    return result.reshape(steps, step_rows, width)


def solution(mesh):
    return jax.shard_map(
        local,
        mesh=mesh,
        in_specs=(
            P(None, ("groups", "hst", "rep"), "mp"),
            P("hst", None, "mp"),
            P("hst", None, "mp"),
            P("groups"),
            P("groups"),
            P(None, ("groups", "hst", "rep"), None),
            P(None, ("groups", "hst", "rep")),
        ),
        out_specs=P(None, ("groups", "hst", "rep"), "mp"),
        check_vma=False,
    )
```

```python
import functools

import jax
import jax.numpy as jnp
from jax import lax
from jax.experimental import pallas as pl
from jax.experimental.pallas import tpu as pltpu
from jax.sharding import PartitionSpec as P

MOST_PAIRED = 8
LANES = 128
VMEM_BYTES = 32 << 20


def round_up(value, unit):
    return unit * -(-value // unit)


def block_names(block):
    count = block.shape[0]
    lane = lax.broadcasted_iota(jnp.int32, (count, LANES), 1)
    row = lax.broadcasted_iota(jnp.int32, (count, LANES), 0)
    last = block[count - 1 :, :LANES].astype(jnp.float32)
    return jnp.sum(
        jnp.where((lane == row) & (row < count - 1), last, 0.0), axis=1, keepdims=True
    )


def lane_adapter(first, rank_extent):
    lane = lax.broadcasted_iota(jnp.int32, (1, LANES), 1)
    return (first + lane // rank_extent + 1).astype(jnp.float32)


def shrink_kernel(counts, own, pieces, rank_extent, first_ref, *refs):
    blocks, refs = refs[: len(counts)], refs[len(counts) :]
    own_names = None
    if own:
        own_names, refs = refs[0], refs[1:]
    weights, (partial_ref, names_ref) = refs[:pieces], refs[pieces:]
    offset = 0
    for index, count in enumerate(counts):
        rows = blocks[index][...]
        names = own_names[...] if own and index == 0 else block_names(rows)
        total = jnp.zeros((count, LANES), jnp.float32)
        number = 0
        for weight in weights:
            for start in range(0, weight.shape[0], LANES):
                product = lax.dot_general(
                    rows,
                    weight[start : start + LANES, :],
                    (((1,), (1,)), ((), ())),
                    preferred_element_type=jnp.float32,
                )
                here = names == lane_adapter(first_ref[number], rank_extent)
                total = total + jnp.where(here, product, 0.0)
                number += 1
        partial_ref[offset : offset + count, :] = total
        names_ref[offset : offset + count, :] = jnp.broadcast_to(names, (count, LANES))
        offset += count


def expand_kernel(counts, shares, pieces, rank_extent, told, first_ref, *refs):
    if told:
        told_ref, refs = refs[0], refs[1:]
    partials, refs = refs[:shares], refs[shares:]
    names_ref, refs = refs[0], refs[1:]
    weights, refs = refs[:pieces], refs[pieces:]
    outs, spread_ref = refs[:-1], refs[-1]

    @pl.when(pl.program_id(0) == 0)
    def _():
        total = partials[0][...]
        for partial in partials[1:]:
            total = total + partial[...]
        shrink = total.astype(jnp.bfloat16).astype(jnp.float32)
        for number in range(spread_ref.shape[1] // LANES):
            here = names_ref[...] == lane_adapter(first_ref[number], rank_extent)
            spread_ref[:, number * LANES : (number + 1) * LANES] = jnp.where(
                here, shrink, 0.0
            ).astype(jnp.bfloat16)

    total = None
    column = 0
    for weight in weights:
        depth = weight.shape[0]
        product = jnp.dot(
            spread_ref[:, column : column + depth],
            weight[...],
            preferred_element_type=jnp.float32,
        )
        total = product if total is None else total + product
        column += depth
    offset = 0
    for count, out in zip(counts, outs):
        values = total[offset : offset + count, :]
        if told:
            row = lax.broadcasted_iota(jnp.int32, values.shape, 0)
            values = jnp.where(row == count - 1, told_ref[0].astype(jnp.float32), values)
        out[...] = values.astype(out.dtype)
        offset += count


def column_of(line, where):
    return jnp.sum(jnp.where(where, line, 0), axis=1, keepdims=True)


def as_line(column):
    shape = (column.shape[0], LANES)
    turn = lax.broadcasted_iota(jnp.int32, shape, 0) == lax.broadcasted_iota(jnp.int32, shape, 1)
    return jnp.sum(jnp.where(turn, column, 0), axis=0, keepdims=True)


def counted(marked):
    lanes = marked.shape[1]
    earlier = lax.broadcasted_iota(jnp.int32, (lanes, lanes), 0) < lax.broadcasted_iota(
        jnp.int32, (lanes, lanes), 1
    )
    return jnp.dot(
        marked.astype(jnp.bfloat16),
        earlier.astype(jnp.bfloat16),
        preferred_element_type=jnp.float32,
    ).astype(jnp.int32)


def put_block(ref, rows, last):
    count = rows.shape[0]
    ref[...] = rows.astype(ref.dtype)
    row = lax.broadcasted_iota(jnp.int32, (count, LANES), 0)
    head = jnp.where(row == count - 1, last.astype(jnp.float32), rows[:, :LANES])
    ref[:, :LANES] = head.astype(ref.dtype)


def slots_of(block, rows):
    return lax.broadcasted_iota(jnp.int32, (block, rows), 0)


def route_kernel(member, local_adapters, me_ref, source_ref, wanted_ref, x_ref, packed_ref, route_ref):
    table = source_ref.shape[1]
    rows = x_ref.shape[0]
    block = packed_ref.shape[0]
    diagonal = lax.broadcasted_iota(jnp.int32, (table, table), 0) == lax.broadcasted_iota(
        jnp.int32, (table, table), 1
    )
    source = column_of(source_ref[...], diagonal)
    entry = lax.broadcasted_iota(jnp.int32, (table, rows), 0)
    served = jnp.sum(jnp.where(entry == wanted_ref[...], source, 0), axis=0, keepdims=True)
    owner = lax.div(served, jnp.int32(local_adapters))
    name = served - owner * local_adapters + 1
    key = owner ^ me_ref[0]
    line = lax.broadcasted_iota(jnp.int32, (8, rows), 0)
    rank = jnp.sum(jnp.where(line == key, counted(line == key), 0), axis=0, keepdims=True)
    route_ref[...] = jnp.where(line == 0, key, jnp.where(line == 1, rank, name))
    slot = slots_of(block, rows)
    chosen = (key == member) & (slot == rank) & (slot < block - 1)
    packed = jnp.dot(chosen.astype(jnp.bfloat16), x_ref[...], preferred_element_type=jnp.float32)
    put_block(packed_ref, packed, as_line(column_of(name, chosen)))


def spill_kernel(far, room, shared, route_ref, x_ref, spill_ref, index_ref):
    rows = x_ref.shape[0]
    block = spill_ref.shape[0]
    key, rank, name = route_ref[0:1, :], route_ref[1:2, :], route_ref[2:3, :]
    spilled = (key >= far) & (rank >= room + shared)
    line = lax.broadcasted_iota(jnp.int32, (8, rows), 0)
    index = counted((line >= 0) & spilled)
    index = jnp.where(spilled, index[0:1, :], -1)
    index_ref[...] = jnp.where(line >= 0, index, 0)
    slot = slots_of(block, rows)
    chosen = (slot == index) & (slot < block - 1)
    code = name + jnp.where(key > far, LANES // 2, 0)
    last = as_line(column_of(code, chosen))
    lane = lax.broadcasted_iota(jnp.int32, (1, LANES), 1)
    for number in range(2):
        free = shared - own_share(key, rank, far + number, room, shared)
        last = jnp.where(lane == LANES // 2 + number, free, last)
    packed = jnp.dot(chosen.astype(jnp.bfloat16), x_ref[...], preferred_element_type=jnp.float32)
    put_block(spill_ref, packed, last)


def own_share(key, rank, member, room, shared):
    held = jnp.max(jnp.where(key == member, rank + 1, 0), axis=1, keepdims=True)
    return jnp.clip(held - room, 0, shared)


def settle_kernel(
    far, room, shared, near_room, more, route_ref, index_ref, x_ref, guest_ref,
    first_ref, second_ref, placed_ref, left_ref, rounds_ref,
):
    rows = x_ref.shape[0]
    block = first_ref.shape[0]
    key, rank, name = route_ref[0:1, :], route_ref[1:2, :], route_ref[2:3, :]
    index = index_ref[0:1, :]
    told = guest_ref[...][block - 1 :, :LANES].astype(jnp.float32).astype(jnp.int32)
    lane = lax.broadcasted_iota(jnp.int32, (1, LANES), 1)
    code = jnp.where(lane < block - 1, told, 0)
    second = code > LANES // 2
    guest_name = code - jnp.where(second, LANES // 2, 0)
    line = lax.broadcasted_iota(jnp.int32, (8, LANES), 0)
    mine = (code > 0) & ((line > 0) == second)
    order = jnp.sum(jnp.where(mine & (line < 2), counted(mine), 0), axis=0, keepdims=True)
    start = jnp.where(key == 0, rows, near_room)
    kept = jnp.full_like(key, -1)
    for number, packed_ref in enumerate((first_ref, second_ref)):
        member = far + number
        share = own_share(key, rank, member, room, shared)
        slot = slots_of(block, rows)
        own = (key == member) & (slot + room == rank) & (slot < block - 1)
        slot = slots_of(block, LANES)
        guest = (code > 0) & (second == (number == 1)) & (slot == order + share) & (slot < block - 1)
        placed_ref[number, :, :] = guest.astype(jnp.float32)
        packed = jnp.dot(own.astype(jnp.bfloat16), x_ref[...], preferred_element_type=jnp.float32)
        packed = packed + jnp.dot(
            guest.astype(jnp.bfloat16)[:, :block], guest_ref[...], preferred_element_type=jnp.float32
        )
        names = column_of(name, own) + column_of(guest_name, guest)
        put_block(packed_ref, packed, as_line(names))
        free = jnp.sum(jnp.where(lane == LANES // 2 + number, told, 0), axis=1, keepdims=True)
        over = rank - (room + shared)
        taken = (key == member) & (over >= 0) & (over < free) & (index < block - 1)
        kept = jnp.where(taken, index, kept)
        reached = room + shared + jnp.max(jnp.where(taken, over + 1, 0), axis=1, keepdims=True)
        start = jnp.where(key == member, reached, start)
    left = rank - start
    line = lax.broadcasted_iota(jnp.int32, (8, rows), 0)
    left_ref[...] = jnp.where(line == 0, left, kept)
    rounds_ref[0] = lax.div(jnp.max(jnp.maximum(left + 1, 0)) + (more - 1), jnp.int32(more))


def hand_kernel(placed_ref, first_ref, second_ref, out_ref):
    total = None
    for number, ref in enumerate((first_ref, second_ref)):
        part = lax.dot_general(
            placed_ref[number, :, :].astype(jnp.bfloat16),
            ref[...],
            (((0,), (0,)), ((), ())),
            preferred_element_type=jnp.float32,
        )
        total = part if total is None else total + part
    out_ref[...] = total[: out_ref.shape[0], :].astype(out_ref.dtype)


def small_call(kernel, outs, scalars, *args):
    whole = pl.BlockSpec(memory_space=pltpu.VMEM)
    scalar = pl.BlockSpec(memory_space=pltpu.SMEM)
    return pl.pallas_call(
        kernel,
        out_shape=[jax.ShapeDtypeStruct(shape, dtype) for shape, dtype in outs],
        in_specs=[scalar] * scalars + [whole] * (len(args) - scalars),
        out_specs=[scalar if shape == (1,) else whole for shape, _ in outs],
        compiler_params=pltpu.CompilerParams(vmem_limit_bytes=VMEM_BYTES),
    )(*args)


def back_kernel(blocks, base_ref, *refs):
    places, returned, outs = refs[:blocks], refs[blocks : 2 * blocks], refs[2 * blocks :]
    out_ref = outs[0]
    total = base_ref[...].astype(jnp.float32)
    for place, block in zip(places, returned):
        total = total + jnp.dot(place[...], block[...], preferred_element_type=jnp.float32)
    out_ref[...] = total.astype(out_ref.dtype)
    if len(outs) == 1:
        return

    @pl.when(pl.program_id(0) == 0)
    def _():
        told = jnp.float32(0)
        for block in returned:
            rows = block[...]
            told = jnp.maximum(told, jnp.max(rows[rows.shape[0] - 1 :, :LANES].astype(jnp.float32)))
        outs[1][0] = told.astype(jnp.int32)


def shrink_call(blocks, own_names, weights, firsts, rank_extent):
    counts = [block.shape[0] for block in blocks]
    rows = sum(counts)
    width = blocks[0].shape[1]
    spots = sum(weight.shape[0] for weight in weights)
    names = [] if own_names is None else [own_names]
    whole = pl.BlockSpec(memory_space=pltpu.VMEM)
    return pl.pallas_call(
        functools.partial(
            shrink_kernel, counts, own_names is not None, len(weights), rank_extent
        ),
        out_shape=(jax.ShapeDtypeStruct((rows, LANES), jnp.float32),) * 2,
        in_specs=[pl.BlockSpec(memory_space=pltpu.SMEM)]
        + [whole] * (len(blocks) + len(names) + len(weights)),
        out_specs=(whole, whole),
        compiler_params=pltpu.CompilerParams(vmem_limit_bytes=VMEM_BYTES),
        cost_estimate=pl.CostEstimate(
            flops=2 * rows * spots * width,
            bytes_accessed=2 * (rows + spots) * width,
            transcendentals=0,
        ),
    )(firsts, *blocks, *names, *weights)


def back_call(base, places, returned, told, weight=1):
    rows, width = base.shape
    tile = width // 6 if width % (6 * LANES) == 0 else width
    tiles = lambda count: pl.BlockSpec((count, tile), lambda i: (0, i))
    return pl.pallas_call(
        functools.partial(back_kernel, len(returned)),
        grid=(width // tile,),
        out_shape=[jax.ShapeDtypeStruct((rows, width), jnp.bfloat16)]
        + [jax.ShapeDtypeStruct((1,), jnp.int32)] * told,
        in_specs=[tiles(rows)]
        + [pl.BlockSpec(place.shape, lambda i: (0, 0)) for place in places]
        + [tiles(block.shape[0]) for block in returned],
        out_specs=[tiles(rows)] + [pl.BlockSpec(memory_space=pltpu.SMEM)] * told,
        compiler_params=pltpu.CompilerParams(vmem_limit_bytes=VMEM_BYTES),
        cost_estimate=pl.CostEstimate(
            flops=2 * weight * rows * width * sum(block.shape[0] for block in returned),
            bytes_accessed=4 * weight * rows * width,
            transcendentals=0,
        ),
    )(base, *places, *returned)


def expand_call(partials, names, weights, firsts, counts, rank_extent, told=None):
    width = weights[0].shape[1]
    rows = names.shape[0]
    spots = sum(weight.shape[0] for weight in weights)
    tile = width // 6 if width % (6 * LANES) == 0 else width
    whole = pl.BlockSpec(memory_space=pltpu.VMEM)
    return pl.pallas_call(
        functools.partial(
            expand_kernel, counts, len(partials), len(weights), rank_extent, told is not None
        ),
        grid=(width // tile,),
        out_shape=[jax.ShapeDtypeStruct((count, width), jnp.bfloat16) for count in counts],
        in_specs=[pl.BlockSpec(memory_space=pltpu.SMEM)] * (1 if told is None else 2)
        + [whole] * (len(partials) + 1)
        + [pl.BlockSpec((weight.shape[0], tile), lambda i: (0, i)) for weight in weights],
        out_specs=[pl.BlockSpec((count, tile), lambda i: (0, i)) for count in counts],
        scratch_shapes=[pltpu.VMEM((rows, spots), jnp.bfloat16)],
        compiler_params=pltpu.CompilerParams(vmem_limit_bytes=VMEM_BYTES),
        cost_estimate=pl.CostEstimate(
            flops=2 * rows * spots * width,
            bytes_accessed=2 * (rows + spots) * width,
            transcendentals=0,
        ),
    )(firsts, *([] if told is None else [told]), *partials, names, *weights)


def local(
    activations,
    shrink_weight,
    expand_weight,
    former_layout_list,
    host_layout_list,
    target_host,
    target_position,
):
    host_count = lax.axis_size("hst")
    shares = lax.axis_size("mp")
    me = lax.axis_index("hst")
    local_adapters, rank_extent, width = shrink_weight.shape
    steps, step_rows, _ = activations.shape
    rows = steps * step_rows
    spots = local_adapters * rank_extent
    folded = LANES if spots % LANES == 0 and LANES % rank_extent == 0 else spots
    table_size = former_layout_list.shape[0]
    paired = host_count <= MOST_PAIRED and host_count & (host_count - 1) == 0
    first_block = round_up(11 * rows // (8 * host_count), 8)
    more_block = min(first_block, 16)

    flat_x = activations.reshape(rows, width)
    flat_a = shrink_weight.reshape(spots, width)
    flat_b = expand_weight.reshape(spots, width)

    table = jnp.arange(table_size, dtype=jnp.int32)
    source = jnp.sum(
        jnp.where(host_layout_list[:, None] == former_layout_list[None, :], table[None, :], 0),
        axis=1,
    )
    wanted = (target_host[:, :, 0] * local_adapters + target_position).reshape(rows)

    def route():
        served = jnp.sum(jnp.where(wanted[:, None] == table[None, :], source[None, :], 0), axis=1)
        owner = served // local_adapters
        key = owner ^ me if paired else jnp.where(owner == me, host_count, owner)
        in_block = key[:, None] == jnp.arange(host_count, dtype=jnp.int32)[None, :]
        row_ids = jnp.arange(rows, dtype=jnp.int32)
        earlier = (row_ids[None, :] < row_ids[:, None]).astype(jnp.bfloat16)
        before = jnp.dot(
            earlier, in_block.astype(jnp.bfloat16), preferred_element_type=jnp.float32
        ).astype(jnp.int32)
        row_rank = jnp.sum(jnp.where(in_block, before, 0), axis=1)
        most = jnp.max(jnp.where(owner == me, 0, row_rank + 1))
        return key, row_rank, served % local_adapters + 1, owner == me, most

    tiled = (
        host_count == 4
        and lax.axis_size("rep") == 2
        and spots % LANES == 0
        and LANES % rank_extent == 0
        and 2 * local_adapters < LANES
    )
    main_block = round_up(rows // host_count, 16)
    shared_block = 16
    if tiled:
        wide = ((main_block, width), jnp.bfloat16)
        first_packed, lines = small_call(
            functools.partial(route_kernel, 2, local_adapters),
            [wide, ((8, rows), jnp.int32)],
            1,
            me.reshape(1),
            source.reshape(1, -1),
            wanted.reshape(1, -1),
            flat_x,
        )
        key, row_rank, named_row = lines[0], lines[1], lines[2]
        stays = key == 0
        own_rounds = 0
    else:
        key, row_rank, named_row, stays, most = route()
        left = most - (first_block - 1)
        own_rounds = jnp.maximum(0, (left + more_block - 2) // (more_block - 1))

    columns = jnp.arange(width, dtype=jnp.int32)
    spot_adapter = jnp.arange(spots, dtype=jnp.int32) // rank_extent + 1

    def place(member, start, block, key, row_rank):
        slot = jnp.arange(block, dtype=jnp.int32)[:, None]
        chosen = (
            (key[None, :] == member)
            & (slot + start == row_rank[None, :])
            & (slot < block - 1)
        )
        return chosen.astype(jnp.bfloat16)

    def pack(member, start, block, key, row_rank, told):
        at_column = (key[:, None] == member) & (row_rank[:, None] == columns[None, :LANES] + start)
        names = jnp.sum(jnp.where(at_column, named_row[:, None], 0), axis=0)
        lane = columns[:LANES]
        names = jnp.where(lane < block - 1, names, jnp.where(lane == block - 1, told, 0))
        names = jnp.pad(names.astype(jnp.float32), (0, width - LANES))
        rows_out = jnp.dot(
            place(member, start, block, key, row_rank),
            flat_x,
            preferred_element_type=jnp.float32,
        )
        last = (jnp.arange(block) == block - 1)[:, None]
        return jnp.where(last, names[None, :], rows_out).astype(jnp.bfloat16)

    def swap(values, step):
        return lax.ppermute(values, "hst", [(i, i ^ step) for i in range(host_count)])

    def exchange(values):
        split = values.reshape(host_count, -1, values.shape[-1])
        split = lax.all_to_all(split, "hst", split_axis=0, concat_axis=0, tiled=True)
        return split.reshape(values.shape)

    def fold(values):
        parts = [values[:, i : i + folded] for i in range(0, spots, folded)]
        total = parts[0]
        for part in parts[1:]:
            total = total + part
        return total

    def adapt(inputs, names):
        mask = names[:, None] == spot_adapter[None, :]
        partial = lax.dot_general(
            inputs, flat_a, (((1,), (1,)), ((), ())), preferred_element_type=jnp.float32
        )
        partial = fold(jnp.where(mask, partial, 0.0))
        total = partial
        for hop in range(1, shares):
            total = total + lax.ppermute(
                partial, "mp", [(i, (i + hop) % shares) for i in range(shares)]
            )
        shrink = jnp.tile(total.astype(jnp.bfloat16), (1, spots // folded))
        spread = jnp.where(mask, shrink, 0)
        return jnp.dot(spread, flat_b, preferred_element_type=jnp.float32)

    def serve(received, block):
        names = received.reshape(-1, block, width)[:, block - 1, :LANES].astype(jnp.int32)
        rounds = jnp.max(names[:, block - 1])
        names = jnp.where(jnp.arange(block)[None, :] < block - 1, names[:, :block], 0)
        return adapt(received, names.reshape(-1)).astype(jnp.bfloat16), rounds

    def back(member, start, block, row_rank, returned):
        return lax.dot_general(
            place(member, start, block, key, row_rank),
            returned,
            (((0,), (0,)), ((), ())),
            preferred_element_type=jnp.float32,
        )

    def one_round(start, block, base, row_rank):
        if not paired:
            packed = jnp.concatenate([pack(member, start, block, key, row_rank, own_rounds) for member in range(host_count)])
            adapted, rounds = serve(exchange(packed), block)
            returned = exchange(adapted).reshape(host_count, block, width)
            for member in range(host_count):
                base = base + back(member, start, block, row_rank, returned[member])
            return base.astype(jnp.bfloat16), jnp.maximum(rounds, own_rounds)
        received = {s: swap(pack(s, start, block, key, row_rank, own_rounds), s) for s in range(1, host_count)}
        rounds = own_rounds
        for s in range(1, host_count):
            adapted, theirs = serve(received[s], block)
            rounds = jnp.maximum(rounds, theirs)
            returned = swap(adapted, s)
            base = (base + back(s, start, block, row_rank, returned)).astype(jnp.bfloat16)
        return base, rounds

    def agree(rounds):
        rounds = jnp.full((1, LANES), rounds, jnp.int32)
        for axis in ("rep", "groups"):
            size = lax.axis_size(axis)
            most = rounds
            for hop in range(1, size):
                most = jnp.maximum(
                    most,
                    lax.ppermute(rounds, axis, [(i, (i + hop) % size) for i in range(size)]),
                )
            rounds = most
        return rounds

    def over_shares(partial):
        return [partial] + [
            lax.ppermute(partial, "mp", [(i, (i + hop) % shares) for i in range(shares)])
            for hop in range(1, shares)
        ]

    def paired_round(key, row_rank):
        firsts = (LANES // rank_extent) * jnp.arange(spots // LANES, dtype=jnp.int32)
        block = first_block

        def shrink(blocks, names):
            return shrink_call(blocks, names, [flat_a], firsts, rank_extent)

        def expand(blocks, partial, names, told=None):
            return expand_call(
                over_shares(partial),
                names,
                [flat_b],
                firsts,
                [rows_in.shape[0] for rows_in in blocks],
                rank_extent,
                told,
            )

        near, first, last = 1, 2, 3
        room, shared = main_block - 1, shared_block - 1
        share = ((shared_block, width), jnp.bfloat16)
        came = {"F": [swap(first_packed, first)]}
        spill, index = small_call(
            functools.partial(spill_kernel, first, room, shared),
            [share, ((8, rows), jnp.int32)],
            0,
            lines,
            flat_x,
        )
        cores = [(0, 1), (1, 0)]
        guests = lax.ppermute(spill, "rep", cores)
        own_names = jnp.where(stays, named_row, 0).astype(jnp.float32)[:, None]
        own_names, _ = lax.optimization_barrier((own_names, spill))
        partial, names = shrink([flat_x], own_names)
        partial, key, row_rank, guests = lax.optimization_barrier((partial, key, row_rank, guests))
        came["L"] = [swap(pack(last, 0, main_block, key, row_rank, 0), last)]
        came["N"] = [swap(pack(near, 0, block, key, row_rank, 0), near)]
        shared_first, shared_last, placed, remaining, rounds = small_call(
            functools.partial(settle_kernel, first, room, shared, block - 1, more_block - 1),
            [
                share,
                share,
                ((2, shared_block, LANES), jnp.float32),
                ((8, rows), jnp.int32),
                ((1,), jnp.int32),
            ],
            0,
            lines,
            index,
            flat_x,
            guests,
        )
        came["b"] = [swap(shared_first, first), swap(shared_last, last)]
        (base,) = expand([flat_x], partial, names)
        rounds = agree(rounds[0])[0]
        across = {"F": [first], "N": [near], "b": [first, last], "L": [last]}
        gone = {}
        order = ['F', 'b', 'N', 'L']
        for number, together in enumerate(order):
            blocks = sum((came[part] for part in together), [])
            partial, names = shrink(blocks, None)
            adapted = expand(blocks, partial, names, None if together == "L" else rounds)
            if number + 1 < len(order):
                for part in order[number + 1]:
                    _, came[part] = lax.optimization_barrier((tuple(adapted), came[part]))
            if together == "L":
                adapted, gone["F"] = lax.optimization_barrier((adapted, gone["F"]))
                adapted, gone["b"] = lax.optimization_barrier((adapted, gone["b"]))
            steps_across = sum((across[part] for part in together), [])
            sent = [swap(values, s) for values, s in zip(adapted, steps_across)]
            for part in together:
                gone[part], sent = sent[: len(across[part])], sent[len(across[part]) :]
        shared_first, shared_last = gone["b"]
        (hosted,) = small_call(hand_kernel, [share], 0, placed, shared_first, shared_last)
        handed = lax.ppermute(hosted, "rep", cores)
        slot = jnp.arange(shared_block, dtype=jnp.int32)[None, :]
        home = (remaining[1][:, None] == slot).astype(jnp.bfloat16)
        base, told = back_call(
            base,
            [
                place(first, 0, main_block, key, row_rank).T,
                place(near, 0, block, key, row_rank).T,
                place(first, room, shared_block, key, row_rank).T,
                place(last, room, shared_block, key, row_rank).T,
                home,
            ],
            gone["F"] + gone["N"] + [shared_first, shared_last, handed],
            True,
            5,
        )
        place_last = place(last, 0, main_block, key, row_rank).T
        base, place_last = lax.optimization_barrier((base, place_last))
        result = jnp.dot(place_last, gone["L"][0], preferred_element_type=jnp.float32)
        result = (result + base).astype(jnp.bfloat16)
        return result, jnp.maximum(told[0], rounds[0]), remaining[0]

    if tiled:
        result, rounds, left_rank = paired_round(key, row_rank)
    else:
        own = adapt(flat_x, jnp.where(stays, named_row, 0)).astype(jnp.bfloat16)
        result, rounds = one_round(0, first_block, own, row_rank)
        rounds = agree(rounds)[0, 0]
        left_rank = row_rank - (first_block - 1)
    def more(state):
        number, so_far = state
        start = number * (more_block - 1)
        so_far, _ = one_round(start, more_block, so_far, left_rank)
        return number + 1, so_far

    _, result = lax.while_loop(
        lambda state: state[0] < rounds, more, (jnp.int32(0), result)
    )
    return result.reshape(steps, step_rows, width)


def solution(mesh):
    return jax.shard_map(
        local,
        mesh=mesh,
        in_specs=(
            P(None, ("groups", "hst", "rep"), "mp"),
            P("hst", None, "mp"),
            P("hst", None, "mp"),
            P("groups"),
            P("groups"),
            P(None, ("groups", "hst", "rep"), None),
            P(None, ("groups", "hst", "rep")),
        ),
        out_specs=P(None, ("groups", "hst", "rep"), "mp"),
        check_vma=False,
    )
```

```python
import functools

import jax
import jax.numpy as jnp
from jax import lax
from jax.experimental import pallas as pl
from jax.experimental.pallas import tpu as pltpu
from jax.sharding import PartitionSpec as P

MOST_PAIRED = 8
LANES = 128
VMEM_BYTES = 32 << 20


def round_up(value, unit):
    return unit * -(-value // unit)


def block_names(block):
    count = block.shape[0]
    lane = lax.broadcasted_iota(jnp.int32, (count, LANES), 1)
    row = lax.broadcasted_iota(jnp.int32, (count, LANES), 0)
    last = block[count - 1 :, :LANES].astype(jnp.float32)
    return jnp.sum(
        jnp.where((lane == row) & (row < count - 1), last, 0.0), axis=1, keepdims=True
    )


def lane_adapter(first, rank_extent):
    lane = lax.broadcasted_iota(jnp.int32, (1, LANES), 1)
    return (first + lane // rank_extent + 1).astype(jnp.float32)


def shrink_kernel(counts, own, pieces, rank_extent, first_ref, *refs):
    blocks, refs = refs[: len(counts)], refs[len(counts) :]
    own_names = None
    if own:
        own_names, refs = refs[0], refs[1:]
    weights, (partial_ref, names_ref) = refs[:pieces], refs[pieces:]
    offset = 0
    for index, count in enumerate(counts):
        rows = blocks[index][...]
        names = own_names[...] if own and index == 0 else block_names(rows)
        total = jnp.zeros((count, LANES), jnp.float32)
        number = 0
        for weight in weights:
            for start in range(0, weight.shape[0], LANES):
                product = lax.dot_general(
                    rows,
                    weight[start : start + LANES, :],
                    (((1,), (1,)), ((), ())),
                    preferred_element_type=jnp.float32,
                )
                here = names == lane_adapter(first_ref[number], rank_extent)
                total = total + jnp.where(here, product, 0.0)
                number += 1
        partial_ref[offset : offset + count, :] = total
        names_ref[offset : offset + count, :] = jnp.broadcast_to(names, (count, LANES))
        offset += count


def expand_kernel(counts, shares, pieces, rank_extent, told, first_ref, *refs):
    if told:
        told_ref, refs = refs[0], refs[1:]
    partials, refs = refs[:shares], refs[shares:]
    names_ref, refs = refs[0], refs[1:]
    weights, refs = refs[:pieces], refs[pieces:]
    outs, spread_ref = refs[:-1], refs[-1]

    @pl.when(pl.program_id(0) == 0)
    def _():
        total = partials[0][...]
        for partial in partials[1:]:
            total = total + partial[...]
        shrink = total.astype(jnp.bfloat16).astype(jnp.float32)
        for number in range(spread_ref.shape[1] // LANES):
            here = names_ref[...] == lane_adapter(first_ref[number], rank_extent)
            spread_ref[:, number * LANES : (number + 1) * LANES] = jnp.where(
                here, shrink, 0.0
            ).astype(jnp.bfloat16)

    total = None
    column = 0
    for weight in weights:
        depth = weight.shape[0]
        product = jnp.dot(
            spread_ref[:, column : column + depth],
            weight[...],
            preferred_element_type=jnp.float32,
        )
        total = product if total is None else total + product
        column += depth
    offset = 0
    for count, out in zip(counts, outs):
        values = total[offset : offset + count, :]
        if told:
            row = lax.broadcasted_iota(jnp.int32, values.shape, 0)
            values = jnp.where(row == count - 1, told_ref[0].astype(jnp.float32), values)
        out[...] = values.astype(out.dtype)
        offset += count


def column_of(line, where):
    return jnp.sum(jnp.where(where, line, 0), axis=1, keepdims=True)


def as_line(column):
    shape = (column.shape[0], LANES)
    turn = lax.broadcasted_iota(jnp.int32, shape, 0) == lax.broadcasted_iota(jnp.int32, shape, 1)
    return jnp.sum(jnp.where(turn, column, 0), axis=0, keepdims=True)


def counted(marked):
    lanes = marked.shape[1]
    earlier = lax.broadcasted_iota(jnp.int32, (lanes, lanes), 0) < lax.broadcasted_iota(
        jnp.int32, (lanes, lanes), 1
    )
    return jnp.dot(
        marked.astype(jnp.bfloat16),
        earlier.astype(jnp.bfloat16),
        preferred_element_type=jnp.float32,
    ).astype(jnp.int32)


def put_block(ref, rows, last):
    count = rows.shape[0]
    ref[...] = rows.astype(ref.dtype)
    row = lax.broadcasted_iota(jnp.int32, (count, LANES), 0)
    head = jnp.where(row == count - 1, last.astype(jnp.float32), rows[:, :LANES])
    ref[:, :LANES] = head.astype(ref.dtype)


def slots_of(block, rows):
    return lax.broadcasted_iota(jnp.int32, (block, rows), 0)


def route_kernel(member, local_adapters, me_ref, source_ref, wanted_ref, x_ref, packed_ref, route_ref):
    table = source_ref.shape[1]
    rows = x_ref.shape[0]
    block = packed_ref.shape[0]
    diagonal = lax.broadcasted_iota(jnp.int32, (table, table), 0) == lax.broadcasted_iota(
        jnp.int32, (table, table), 1
    )
    source = column_of(source_ref[...], diagonal)
    entry = lax.broadcasted_iota(jnp.int32, (table, rows), 0)
    served = jnp.sum(jnp.where(entry == wanted_ref[...], source, 0), axis=0, keepdims=True)
    owner = lax.div(served, jnp.int32(local_adapters))
    name = served - owner * local_adapters + 1
    key = owner ^ me_ref[0]
    line = lax.broadcasted_iota(jnp.int32, (8, rows), 0)
    rank = jnp.sum(jnp.where(line == key, counted(line == key), 0), axis=0, keepdims=True)
    route_ref[...] = jnp.where(line == 0, key, jnp.where(line == 1, rank, name))
    slot = slots_of(block, rows)
    chosen = (key == member) & (slot == rank) & (slot < block - 1)
    packed = jnp.dot(chosen.astype(jnp.bfloat16), x_ref[...], preferred_element_type=jnp.float32)
    put_block(packed_ref, packed, as_line(column_of(name, chosen)))


def spill_kernel(far, room, shared, route_ref, x_ref, spill_ref, index_ref):
    rows = x_ref.shape[0]
    block = spill_ref.shape[0]
    key, rank, name = route_ref[0:1, :], route_ref[1:2, :], route_ref[2:3, :]
    spilled = (key >= far) & (rank >= room + shared)
    line = lax.broadcasted_iota(jnp.int32, (8, rows), 0)
    index = counted((line >= 0) & spilled)
    index = jnp.where(spilled, index[0:1, :], -1)
    index_ref[...] = jnp.where(line >= 0, index, 0)
    slot = slots_of(block, rows)
    chosen = (slot == index) & (slot < block - 1)
    code = name + jnp.where(key > far, LANES // 2, 0)
    last = as_line(column_of(code, chosen))
    lane = lax.broadcasted_iota(jnp.int32, (1, LANES), 1)
    for number in range(2):
        free = shared - own_share(key, rank, far + number, room, shared)
        last = jnp.where(lane == LANES // 2 + number, free, last)
    packed = jnp.dot(chosen.astype(jnp.bfloat16), x_ref[...], preferred_element_type=jnp.float32)
    put_block(spill_ref, packed, last)


def own_share(key, rank, member, room, shared):
    held = jnp.max(jnp.where(key == member, rank + 1, 0), axis=1, keepdims=True)
    return jnp.clip(held - room, 0, shared)


def settle_kernel(
    far, room, shared, near_room, more, route_ref, index_ref, x_ref, guest_ref,
    first_ref, second_ref, placed_ref, left_ref, rounds_ref,
):
    rows = x_ref.shape[0]
    block = first_ref.shape[0]
    key, rank, name = route_ref[0:1, :], route_ref[1:2, :], route_ref[2:3, :]
    index = index_ref[0:1, :]
    told = guest_ref[...][block - 1 :, :LANES].astype(jnp.float32).astype(jnp.int32)
    lane = lax.broadcasted_iota(jnp.int32, (1, LANES), 1)
    code = jnp.where(lane < block - 1, told, 0)
    second = code > LANES // 2
    guest_name = code - jnp.where(second, LANES // 2, 0)
    line = lax.broadcasted_iota(jnp.int32, (8, LANES), 0)
    mine = (code > 0) & ((line > 0) == second)
    order = jnp.sum(jnp.where(mine & (line < 2), counted(mine), 0), axis=0, keepdims=True)
    start = jnp.where(key == 0, rows, near_room)
    kept = jnp.full_like(key, -1)
    for number, packed_ref in enumerate((first_ref, second_ref)):
        member = far + number
        share = own_share(key, rank, member, room, shared)
        slot = slots_of(block, rows)
        own = (key == member) & (slot + room == rank) & (slot < block - 1)
        slot = slots_of(block, LANES)
        guest = (code > 0) & (second == (number == 1)) & (slot == order + share) & (slot < block - 1)
        placed_ref[number, :, :] = guest.astype(jnp.float32)
        packed = jnp.dot(own.astype(jnp.bfloat16), x_ref[...], preferred_element_type=jnp.float32)
        packed = packed + jnp.dot(
            guest.astype(jnp.bfloat16)[:, :block], guest_ref[...], preferred_element_type=jnp.float32
        )
        names = column_of(name, own) + column_of(guest_name, guest)
        put_block(packed_ref, packed, as_line(names))
        free = jnp.sum(jnp.where(lane == LANES // 2 + number, told, 0), axis=1, keepdims=True)
        over = rank - (room + shared)
        taken = (key == member) & (over >= 0) & (over < free) & (index < block - 1)
        kept = jnp.where(taken, index, kept)
        reached = room + shared + jnp.max(jnp.where(taken, over + 1, 0), axis=1, keepdims=True)
        start = jnp.where(key == member, reached, start)
    left = rank - start
    line = lax.broadcasted_iota(jnp.int32, (8, rows), 0)
    left_ref[...] = jnp.where(line == 0, left, kept)
    rounds_ref[0] = lax.div(jnp.max(jnp.maximum(left + 1, 0)) + (more - 1), jnp.int32(more))


def hand_kernel(placed_ref, first_ref, second_ref, out_ref):
    total = None
    for number, ref in enumerate((first_ref, second_ref)):
        part = lax.dot_general(
            placed_ref[number, :, :].astype(jnp.bfloat16),
            ref[...],
            (((0,), (0,)), ((), ())),
            preferred_element_type=jnp.float32,
        )
        total = part if total is None else total + part
    out_ref[...] = total[: out_ref.shape[0], :].astype(out_ref.dtype)


def small_call(kernel, outs, scalars, *args):
    whole = pl.BlockSpec(memory_space=pltpu.VMEM)
    scalar = pl.BlockSpec(memory_space=pltpu.SMEM)
    return pl.pallas_call(
        kernel,
        out_shape=[jax.ShapeDtypeStruct(shape, dtype) for shape, dtype in outs],
        in_specs=[scalar] * scalars + [whole] * (len(args) - scalars),
        out_specs=[scalar if shape == (1,) else whole for shape, _ in outs],
        compiler_params=pltpu.CompilerParams(vmem_limit_bytes=VMEM_BYTES),
    )(*args)


def back_kernel(blocks, base_ref, *refs):
    places, returned, outs = refs[:blocks], refs[blocks : 2 * blocks], refs[2 * blocks :]
    out_ref = outs[0]
    total = base_ref[...].astype(jnp.float32)
    for place, block in zip(places, returned):
        total = total + jnp.dot(place[...], block[...], preferred_element_type=jnp.float32)
    out_ref[...] = total.astype(out_ref.dtype)
    if len(outs) == 1:
        return

    @pl.when(pl.program_id(0) == 0)
    def _():
        told = jnp.float32(0)
        for block in returned:
            rows = block[...]
            told = jnp.maximum(told, jnp.max(rows[rows.shape[0] - 1 :, :LANES].astype(jnp.float32)))
        outs[1][0] = told.astype(jnp.int32)


def shrink_call(blocks, own_names, weights, firsts, rank_extent):
    counts = [block.shape[0] for block in blocks]
    rows = sum(counts)
    width = blocks[0].shape[1]
    spots = sum(weight.shape[0] for weight in weights)
    names = [] if own_names is None else [own_names]
    whole = pl.BlockSpec(memory_space=pltpu.VMEM)
    return pl.pallas_call(
        functools.partial(
            shrink_kernel, counts, own_names is not None, len(weights), rank_extent
        ),
        out_shape=(jax.ShapeDtypeStruct((rows, LANES), jnp.float32),) * 2,
        in_specs=[pl.BlockSpec(memory_space=pltpu.SMEM)]
        + [whole] * (len(blocks) + len(names) + len(weights)),
        out_specs=(whole, whole),
        compiler_params=pltpu.CompilerParams(vmem_limit_bytes=VMEM_BYTES),
        cost_estimate=pl.CostEstimate(
            flops=2 * rows * spots * width,
            bytes_accessed=2 * (rows + spots) * width,
            transcendentals=0,
        ),
    )(firsts, *blocks, *names, *weights)


def back_call(base, places, returned, told, weight=1):
    rows, width = base.shape
    tile = width // 3 if width % (3 * LANES) == 0 else width
    tiles = lambda count: pl.BlockSpec((count, tile), lambda i: (0, i))
    return pl.pallas_call(
        functools.partial(back_kernel, len(returned)),
        grid=(width // tile,),
        out_shape=[jax.ShapeDtypeStruct((rows, width), jnp.bfloat16)]
        + [jax.ShapeDtypeStruct((1,), jnp.int32)] * told,
        in_specs=[tiles(rows)]
        + [pl.BlockSpec(place.shape, lambda i: (0, 0)) for place in places]
        + [tiles(block.shape[0]) for block in returned],
        out_specs=[tiles(rows)] + [pl.BlockSpec(memory_space=pltpu.SMEM)] * told,
        compiler_params=pltpu.CompilerParams(vmem_limit_bytes=VMEM_BYTES),
        cost_estimate=pl.CostEstimate(
            flops=2 * weight * rows * width * sum(block.shape[0] for block in returned),
            bytes_accessed=4 * weight * rows * width,
            transcendentals=0,
        ),
    )(base, *places, *returned)


def expand_call(partials, names, weights, firsts, counts, rank_extent, told=None):
    width = weights[0].shape[1]
    rows = names.shape[0]
    spots = sum(weight.shape[0] for weight in weights)
    tile = width // 3 if width % (3 * LANES) == 0 else width
    whole = pl.BlockSpec(memory_space=pltpu.VMEM)
    return pl.pallas_call(
        functools.partial(
            expand_kernel, counts, len(partials), len(weights), rank_extent, told is not None
        ),
        grid=(width // tile,),
        out_shape=[jax.ShapeDtypeStruct((count, width), jnp.bfloat16) for count in counts],
        in_specs=[pl.BlockSpec(memory_space=pltpu.SMEM)] * (1 if told is None else 2)
        + [whole] * (len(partials) + 1)
        + [pl.BlockSpec((weight.shape[0], tile), lambda i: (0, i)) for weight in weights],
        out_specs=[pl.BlockSpec((count, tile), lambda i: (0, i)) for count in counts],
        scratch_shapes=[pltpu.VMEM((rows, spots), jnp.bfloat16)],
        compiler_params=pltpu.CompilerParams(vmem_limit_bytes=VMEM_BYTES),
        cost_estimate=pl.CostEstimate(
            flops=2 * rows * spots * width,
            bytes_accessed=2 * (rows + spots) * width,
            transcendentals=0,
        ),
    )(firsts, *([] if told is None else [told]), *partials, names, *weights)


def local(
    activations,
    shrink_weight,
    expand_weight,
    former_layout_list,
    host_layout_list,
    target_host,
    target_position,
):
    host_count = lax.axis_size("hst")
    shares = lax.axis_size("mp")
    me = lax.axis_index("hst")
    local_adapters, rank_extent, width = shrink_weight.shape
    steps, step_rows, _ = activations.shape
    rows = steps * step_rows
    spots = local_adapters * rank_extent
    folded = LANES if spots % LANES == 0 and LANES % rank_extent == 0 else spots
    table_size = former_layout_list.shape[0]
    paired = host_count <= MOST_PAIRED and host_count & (host_count - 1) == 0
    first_block = round_up(11 * rows // (8 * host_count), 8)
    more_block = min(first_block, 16)

    flat_x = activations.reshape(rows, width)
    flat_a = shrink_weight.reshape(spots, width)
    flat_b = expand_weight.reshape(spots, width)

    table = jnp.arange(table_size, dtype=jnp.int32)
    source = jnp.sum(
        jnp.where(host_layout_list[:, None] == former_layout_list[None, :], table[None, :], 0),
        axis=1,
    )
    wanted = (target_host[:, :, 0] * local_adapters + target_position).reshape(rows)

    def route():
        served = jnp.sum(jnp.where(wanted[:, None] == table[None, :], source[None, :], 0), axis=1)
        owner = served // local_adapters
        key = owner ^ me if paired else jnp.where(owner == me, host_count, owner)
        in_block = key[:, None] == jnp.arange(host_count, dtype=jnp.int32)[None, :]
        row_ids = jnp.arange(rows, dtype=jnp.int32)
        earlier = (row_ids[None, :] < row_ids[:, None]).astype(jnp.bfloat16)
        before = jnp.dot(
            earlier, in_block.astype(jnp.bfloat16), preferred_element_type=jnp.float32
        ).astype(jnp.int32)
        row_rank = jnp.sum(jnp.where(in_block, before, 0), axis=1)
        most = jnp.max(jnp.where(owner == me, 0, row_rank + 1))
        return key, row_rank, served % local_adapters + 1, owner == me, most

    tiled = (
        host_count == 4
        and lax.axis_size("rep") == 2
        and spots % LANES == 0
        and LANES % rank_extent == 0
        and 2 * local_adapters < LANES
    )
    main_block = round_up(rows // host_count, 16)
    shared_block = 16
    if tiled:
        wide = ((main_block, width), jnp.bfloat16)
        first_packed, lines = small_call(
            functools.partial(route_kernel, 2, local_adapters),
            [wide, ((8, rows), jnp.int32)],
            1,
            me.reshape(1),
            source.reshape(1, -1),
            wanted.reshape(1, -1),
            flat_x,
        )
        key, row_rank, named_row = lines[0], lines[1], lines[2]
        stays = key == 0
        own_rounds = 0
    else:
        key, row_rank, named_row, stays, most = route()
        left = most - (first_block - 1)
        own_rounds = jnp.maximum(0, (left + more_block - 2) // (more_block - 1))

    columns = jnp.arange(width, dtype=jnp.int32)
    spot_adapter = jnp.arange(spots, dtype=jnp.int32) // rank_extent + 1

    def place(member, start, block, key, row_rank):
        slot = jnp.arange(block, dtype=jnp.int32)[:, None]
        chosen = (
            (key[None, :] == member)
            & (slot + start == row_rank[None, :])
            & (slot < block - 1)
        )
        return chosen.astype(jnp.bfloat16)

    def pack(member, start, block, key, row_rank, told):
        at_column = (key[:, None] == member) & (row_rank[:, None] == columns[None, :LANES] + start)
        names = jnp.sum(jnp.where(at_column, named_row[:, None], 0), axis=0)
        lane = columns[:LANES]
        names = jnp.where(lane < block - 1, names, jnp.where(lane == block - 1, told, 0))
        names = jnp.pad(names.astype(jnp.float32), (0, width - LANES))
        rows_out = jnp.dot(
            place(member, start, block, key, row_rank),
            flat_x,
            preferred_element_type=jnp.float32,
        )
        last = (jnp.arange(block) == block - 1)[:, None]
        return jnp.where(last, names[None, :], rows_out).astype(jnp.bfloat16)

    def swap(values, step):
        return lax.ppermute(values, "hst", [(i, i ^ step) for i in range(host_count)])

    def exchange(values):
        split = values.reshape(host_count, -1, values.shape[-1])
        split = lax.all_to_all(split, "hst", split_axis=0, concat_axis=0, tiled=True)
        return split.reshape(values.shape)

    def fold(values):
        parts = [values[:, i : i + folded] for i in range(0, spots, folded)]
        total = parts[0]
        for part in parts[1:]:
            total = total + part
        return total

    def adapt(inputs, names):
        mask = names[:, None] == spot_adapter[None, :]
        partial = lax.dot_general(
            inputs, flat_a, (((1,), (1,)), ((), ())), preferred_element_type=jnp.float32
        )
        partial = fold(jnp.where(mask, partial, 0.0))
        total = partial
        for hop in range(1, shares):
            total = total + lax.ppermute(
                partial, "mp", [(i, (i + hop) % shares) for i in range(shares)]
            )
        shrink = jnp.tile(total.astype(jnp.bfloat16), (1, spots // folded))
        spread = jnp.where(mask, shrink, 0)
        return jnp.dot(spread, flat_b, preferred_element_type=jnp.float32)

    def serve(received, block):
        names = received.reshape(-1, block, width)[:, block - 1, :LANES].astype(jnp.int32)
        rounds = jnp.max(names[:, block - 1])
        names = jnp.where(jnp.arange(block)[None, :] < block - 1, names[:, :block], 0)
        return adapt(received, names.reshape(-1)).astype(jnp.bfloat16), rounds

    def back(member, start, block, row_rank, returned):
        return lax.dot_general(
            place(member, start, block, key, row_rank),
            returned,
            (((0,), (0,)), ((), ())),
            preferred_element_type=jnp.float32,
        )

    def one_round(start, block, base, row_rank):
        if not paired:
            packed = jnp.concatenate([pack(member, start, block, key, row_rank, own_rounds) for member in range(host_count)])
            adapted, rounds = serve(exchange(packed), block)
            returned = exchange(adapted).reshape(host_count, block, width)
            for member in range(host_count):
                base = base + back(member, start, block, row_rank, returned[member])
            return base.astype(jnp.bfloat16), jnp.maximum(rounds, own_rounds)
        received = {s: swap(pack(s, start, block, key, row_rank, own_rounds), s) for s in range(1, host_count)}
        rounds = own_rounds
        for s in range(1, host_count):
            adapted, theirs = serve(received[s], block)
            rounds = jnp.maximum(rounds, theirs)
            returned = swap(adapted, s)
            base = (base + back(s, start, block, row_rank, returned)).astype(jnp.bfloat16)
        return base, rounds

    def agree(rounds):
        rounds = jnp.full((1, LANES), rounds, jnp.int32)
        for axis in ("rep", "groups"):
            size = lax.axis_size(axis)
            most = rounds
            for hop in range(1, size):
                most = jnp.maximum(
                    most,
                    lax.ppermute(rounds, axis, [(i, (i + hop) % size) for i in range(size)]),
                )
            rounds = most
        return rounds

    def over_shares(partial):
        return [partial] + [
            lax.ppermute(partial, "mp", [(i, (i + hop) % shares) for i in range(shares)])
            for hop in range(1, shares)
        ]

    def paired_round(key, row_rank):
        firsts = (LANES // rank_extent) * jnp.arange(spots // LANES, dtype=jnp.int32)
        block = first_block

        def shrink(blocks, names):
            return shrink_call(blocks, names, [flat_a], firsts, rank_extent)

        def expand(blocks, partial, names, told=None):
            return expand_call(
                over_shares(partial),
                names,
                [flat_b],
                firsts,
                [rows_in.shape[0] for rows_in in blocks],
                rank_extent,
                told,
            )

        near, first, last = 1, 2, 3
        room, shared = main_block - 1, shared_block - 1
        share = ((shared_block, width), jnp.bfloat16)
        came = {"F": [swap(first_packed, first)]}
        spill, index = small_call(
            functools.partial(spill_kernel, first, room, shared),
            [share, ((8, rows), jnp.int32)],
            0,
            lines,
            flat_x,
        )
        cores = [(0, 1), (1, 0)]
        guests = lax.ppermute(spill, "rep", cores)
        own_names = jnp.where(stays, named_row, 0).astype(jnp.float32)[:, None]
        own_names, _ = lax.optimization_barrier((own_names, spill))
        partial, names = shrink([flat_x], own_names)
        partial, key, row_rank, guests = lax.optimization_barrier((partial, key, row_rank, guests))
        packed, guests = lax.optimization_barrier(
            (pack(last, 0, main_block, key, row_rank, 0), guests)
        )
        came["L"] = [swap(packed, last)]
        came["N"] = [swap(pack(near, 0, block, key, row_rank, 0), near)]
        shared_first, shared_last, placed, remaining, rounds = small_call(
            functools.partial(settle_kernel, first, room, shared, block - 1, more_block - 1),
            [
                share,
                share,
                ((2, shared_block, LANES), jnp.float32),
                ((8, rows), jnp.int32),
                ((1,), jnp.int32),
            ],
            0,
            lines,
            index,
            flat_x,
            guests,
        )
        came["b"] = [swap(shared_first, first), swap(shared_last, last)]
        (base,) = expand([flat_x], partial, names)
        rounds = agree(rounds[0])[0]
        across = {"F": [first], "N": [near], "b": [first, last], "L": [last]}
        gone = {}
        order = ['F', 'b', 'N', 'L']
        for number, together in enumerate(order):
            blocks = sum((came[part] for part in together), [])
            partial, names = shrink(blocks, None)
            adapted = expand(blocks, partial, names, None if together == "L" else rounds)
            if number + 1 < len(order):
                for part in order[number + 1]:
                    _, came[part] = lax.optimization_barrier((tuple(adapted), came[part]))
            if together == "L":
                adapted, gone["F"] = lax.optimization_barrier((adapted, gone["F"]))
                adapted, gone["b"] = lax.optimization_barrier((adapted, gone["b"]))
            steps_across = sum((across[part] for part in together), [])
            sent = [swap(values, s) for values, s in zip(adapted, steps_across)]
            for part in together:
                gone[part], sent = sent[: len(across[part])], sent[len(across[part]) :]
        shared_first, shared_last = gone["b"]
        (hosted,) = small_call(hand_kernel, [share], 0, placed, shared_first, shared_last)
        handed = lax.ppermute(hosted, "rep", cores)
        slot = jnp.arange(shared_block, dtype=jnp.int32)[None, :]
        home = (remaining[1][:, None] == slot).astype(jnp.bfloat16)
        base, told = back_call(
            base,
            [
                place(first, 0, main_block, key, row_rank).T,
                place(near, 0, block, key, row_rank).T,
                place(first, room, shared_block, key, row_rank).T,
                place(last, room, shared_block, key, row_rank).T,
                home,
            ],
            gone["F"] + gone["N"] + [shared_first, shared_last, handed],
            True,
            5,
        )
        place_last = place(last, 0, main_block, key, row_rank).T
        base, place_last = lax.optimization_barrier((base, place_last))
        result = jnp.dot(place_last, gone["L"][0], preferred_element_type=jnp.float32)
        result = (result + base).astype(jnp.bfloat16)
        return result, jnp.maximum(told[0], rounds[0]), remaining[0]

    if tiled:
        result, rounds, left_rank = paired_round(key, row_rank)
    else:
        own = adapt(flat_x, jnp.where(stays, named_row, 0)).astype(jnp.bfloat16)
        result, rounds = one_round(0, first_block, own, row_rank)
        rounds = agree(rounds)[0, 0]
        left_rank = row_rank - (first_block - 1)
    def more(state):
        number, so_far = state
        start = number * (more_block - 1)
        so_far, _ = one_round(start, more_block, so_far, left_rank)
        return number + 1, so_far

    _, result = lax.while_loop(
        lambda state: state[0] < rounds, more, (jnp.int32(0), result)
    )
    return result.reshape(steps, step_rows, width)


def solution(mesh):
    return jax.shard_map(
        local,
        mesh=mesh,
        in_specs=(
            P(None, ("groups", "hst", "rep"), "mp"),
            P("hst", None, "mp"),
            P("hst", None, "mp"),
            P("groups"),
            P("groups"),
            P(None, ("groups", "hst", "rep"), None),
            P(None, ("groups", "hst", "rep")),
        ),
        out_specs=P(None, ("groups", "hst", "rep"), "mp"),
        check_vma=False,
    )
```
